128 devices in a mesh: lon: 16 (over z_hi, x, core), lat: 8 (over y, z_lo).
Axes of the slice: x: 4, y: 4, z: 4 (z_hi: 2, z_lo: 2; z = z_hi * 2 + z_lo), core: 2. Of those that a mesh axis runs over, the one named last changes fastest.
Arguments:
- tokens: bfloat16 [3, 16, 512, 1024], P(None, 'lat', 'lon'), may hold values from -48 to 48
- targets: bfloat16 [3, 16, 512, 1024], P(None, 'lat', 'lon'), may hold values from -48 to 48
- w_query: bfloat16 [1024, 1024], replicated, may hold values from -0.1875 to 0.1875
- w_key: bfloat16 [1024, 1024], replicated, may hold values from -0.1875 to 0.1875
- w_value: bfloat16 [1024, 1024], replicated, may hold values from -0.1875 to 0.1875
- w_out: bfloat16 [1024, 1024], replicated, may hold values from -0.1875 to 0.1875
- window_reach: int32 [8], replicated, may hold values from 0 to 2, as said below
- loss_table: int32 [4], replicated, may hold values from 1 to 8
Outputs:
- mixed: bfloat16 [3, 16, 512, 1024], P(None, 'lat', 'lon')
- grad_tokens: float32 [3, 16, 512, 1024], P(None, 'lat', 'lon')
- loss: float32 [], replicated
The draws below stay inside these ranges and needn't reach their ends.
Inputs may be any that keep to these rules, and one draw needn't show every extreme that they name: `window_reach`: every head's reach is at most 2, and one head reaches exactly 2.
All inputs are finite; a program needn't handle non-finite values.
Results may differ from the reference program's by a relative error of at most 0.013.
The reference program's roundings to bfloat16 on the way count: a program that leaves them out, or rounds other values in their place, can miss the bound.
Values may be sent and summed in bfloat16 or wider, within the bound.
No kernel may reach another device: no remote copies, remote signals or barrier semaphores. Data moves between devices by JAX's collectives and lax.ppermute only.
A program may use at most 128 MiB of HBM per device.

```python
import math
import jax
import jax.numpy as jnp
from jax import lax

D = 1024
HEADS = 16
GROUPS = 4
LEVELS = 3
COLS_DEV = 32
REACH = 2
ROWS = 16
COLS = 512
N_LON = 16


def draw_tokens(key, part):
    key = jax.random.fold_in(key, 11)
    shape = (LEVELS, ROWS, COLS, D)
    base = jax.random.normal(key, shape, jnp.float32)
    return jnp.clip(base, -6.0, 6.0).astype(jnp.bfloat16)


def ramp_scale(col_factor, row_factor):
    col_pos = jnp.arange(COLS, dtype=jnp.float32) / max(COLS - 1, 1)
    row_pos = jnp.arange(ROWS, dtype=jnp.float32) / max(ROWS - 1, 1)
    logs = row_pos[:, None] * math.log(row_factor) + col_pos[None, :] * math.log(col_factor)
    return jnp.exp(logs)[None, :, :, None]


def draw_targets(key, part):
    key = jax.random.fold_in(key, 23)
    shape = (LEVELS, ROWS, COLS, D)
    base = jnp.clip(jax.random.normal(key, shape, jnp.float32), -6.0, 6.0)
    scaled = base * ramp_scale(3.0, 2.0)
    return jnp.clip(scaled, -48.0, 48.0).astype(jnp.bfloat16)


def draw_window_reach(key, part):
    key = jax.random.fold_in(key, 5)
    count = HEADS // 2
    reach = jax.random.randint(key, (count,), 0, REACH + 1)
    chosen = jax.random.randint(jax.random.fold_in(key, 1), (), 0, count)
    return jnp.where(jnp.arange(count) == chosen, REACH, reach).astype(jnp.int32)


def place_ends(entries, own_key, low, high):
    longest = entries.shape.index(max(entries.shape))
    spots = []
    for shift in (0, 1):
        where = [jax.random.randint(jax.random.fold_in(own_key, axis), (), 0, length) for axis, length in enumerate(entries.shape)]
        where[longest] = (where[longest] + shift) % entries.shape[longest]
        spots.append(tuple(where))
    return entries.at[spots[0]].set(low).at[spots[1]].set(high)


def gaussian(rng, dims, scale, most, held_as=jnp.bfloat16):
    return jnp.clip(scale * jax.random.normal(rng, dims, jnp.float32), -most, most).astype(held_as)


def setup_inputs(seed: int = 0) -> dict:
    streams_of = jax.random.split(jax.random.key(seed), 9)
    tokens = draw_tokens(jax.random.fold_in(streams_of[8], 71), 0)
    targets = draw_targets(jax.random.fold_in(streams_of[8], 71), 0)
    w_query = gaussian(streams_of[2], (D, D), D ** -0.5, 0.1875)
    w_key = gaussian(streams_of[3], (D, D), D ** -0.5, 0.1875)
    w_value = gaussian(streams_of[4], (D, D), D ** -0.5, 0.1875)
    w_out = gaussian(streams_of[5], (D, D), D ** -0.5, 0.1875)
    window_reach = draw_window_reach(jax.random.fold_in(streams_of[8], 71), 0)
    loss_table = place_ends(jax.random.randint(streams_of[7], (GROUPS,), 1, 9), jax.random.fold_in(streams_of[7], 1), 1, 8).astype(jnp.int32)
    return {"tokens": tokens, "targets": targets, "w_query": w_query, "w_key": w_key, "w_value": w_value, "w_out": w_out, "window_reach": window_reach, "loss_table": loss_table}


NEG = -1e+30

def masked_softmax(scores, allowed, axes):
    scores = jnp.where(allowed, scores, NEG)
    top = lax.optimization_barrier(jnp.max(scores, axis=axes, keepdims=True))
    expo = jnp.exp(scores - top)
    return expo / lax.optimization_barrier(jnp.sum(expo, axis=axes, keepdims=True))

def band_row_probs(query, key, scale):
    scores = jnp.einsum('qhd,khd->hqk', query.astype(jnp.float32), key.astype(jnp.float32)) * scale
    top = lax.optimization_barrier(jnp.max(scores, axis=-1, keepdims=True))
    expo = jnp.exp(scores - top)
    return expo / lax.optimization_barrier(jnp.sum(expo, axis=-1, keepdims=True))

def band_forward(query, key, value, scale):
    probs = band_row_probs(query, key, scale)
    weights = probs.astype(jnp.bfloat16)
    return jnp.einsum('hqk,khd->qhd', weights.astype(jnp.float32), value.astype(jnp.float32)).astype(jnp.bfloat16)

def block_sum(terms):
    rounded = lax.optimization_barrier(terms.astype(jnp.bfloat16))
    return lax.optimization_barrier(jnp.sum(rounded.astype(jnp.float32), axis=0)).astype(jnp.bfloat16)

def band_backward(query, key, value, output, d_out, scale):
    half = query.shape[1]
    head_dim = query.shape[2]
    probs = band_row_probs(query, key, scale)
    weights = probs.astype(jnp.bfloat16)
    d_probs = jnp.einsum('qhd,khd->hqk', d_out.astype(jnp.float32), value.astype(jnp.float32))
    delta = lax.optimization_barrier(jnp.sum(d_out.astype(jnp.float32) * output.astype(jnp.float32), axis=-1))
    d_scores = (probs * (d_probs - jnp.transpose(delta)[:, :, None]) * scale).astype(jnp.bfloat16)
    d_query = jnp.einsum('hqk,khd->qhd', d_scores.astype(jnp.float32), key.astype(jnp.float32)).astype(jnp.bfloat16)
    split_scores = d_scores.astype(jnp.float32).reshape(half, N_LON, COLS_DEV, COLS)
    split_weights = weights.astype(jnp.float32).reshape(half, N_LON, COLS_DEV, COLS)
    split_query = query.astype(jnp.float32).reshape(N_LON, COLS_DEV, half, head_dim)
    split_dout = d_out.astype(jnp.float32).reshape(N_LON, COLS_DEV, half, head_dim)
    d_key = block_sum(jnp.einsum('hjqk,jqhd->jkhd', split_scores, split_query))
    d_value = block_sum(jnp.einsum('hjqk,jqhd->jkhd', split_weights, split_dout))
    return (d_query, d_key, d_value)

def window_mask(window_reach):
    span = 2 * REACH + 1
    offset = jnp.arange(span) - REACH
    target = jnp.arange(ROWS)[:, None] + offset[None, :]
    inside = (target >= 0) & (target < ROWS)
    near = jnp.abs(offset)[None, :] <= window_reach[:, None]
    allowed = inside[:, None, :] & near[None, :, :]
    return allowed[None, :, None, :, None, :]

def reference(tokens, targets, w_query, w_key, w_value, w_out, window_reach, loss_table):
    half = HEADS // 2
    head_dim = D // HEADS
    scale = 1.0 / math.sqrt(head_dim)
    count = LEVELS * ROWS * COLS
    flat = tokens.reshape(count, D)
    shape_heads = (LEVELS, ROWS, COLS, HEADS, head_dim)
    queries = jnp.dot(flat, w_query, preferred_element_type=jnp.float32).astype(jnp.bfloat16).reshape(shape_heads)
    keys = jnp.dot(flat, w_key, preferred_element_type=jnp.float32).astype(jnp.bfloat16).reshape(shape_heads)
    values = jnp.dot(flat, w_value, preferred_element_type=jnp.float32).astype(jnp.bfloat16).reshape(shape_heads)
    row_shape = (LEVELS * ROWS, COLS, half, head_dim)
    band_q = queries[..., :half, :].reshape(row_shape)
    band_k = keys[..., :half, :].reshape(row_shape)
    band_v = values[..., :half, :].reshape(row_shape)
    band_out = lax.map(lambda trio: band_forward(trio[0], trio[1], trio[2], scale), (band_q, band_k, band_v))
    window_q = queries[..., half:, :]
    window_k = keys[..., half:, :]
    window_v = values[..., half:, :]
    padding = ((0, 0), (REACH, REACH), (0, 0), (0, 0), (0, 0))
    key_pad = jnp.pad(window_k, padding).astype(jnp.float32)
    value_pad = jnp.pad(window_v, padding).astype(jnp.float32)
    span = 2 * REACH + 1
    query_wide = window_q.astype(jnp.float32)
    scores = jnp.stack([jnp.einsum('lrchd,mrchd->lrchm', query_wide, key_pad[:, shift_row:shift_row + ROWS]) for shift_row in range(span)], axis=-1) * scale
    allowed = window_mask(window_reach)
    window_probs = masked_softmax(scores, allowed, (-2, -1))
    window_weights = window_probs.astype(jnp.bfloat16).astype(jnp.float32)
    window_sum = jnp.zeros(window_q.shape, jnp.float32)
    for shift_row in range(span):
        window_sum = window_sum + jnp.einsum('lrchm,mrchd->lrchd', window_weights[..., shift_row], value_pad[:, shift_row:shift_row + ROWS])
    window_out = window_sum.astype(jnp.bfloat16)
    attended = jnp.concatenate([band_out.reshape(LEVELS, ROWS, COLS, half, head_dim), window_out], axis=3).reshape(count, D)
    mixed = (flat.astype(jnp.float32) + jnp.dot(attended, w_out, preferred_element_type=jnp.float32)).astype(jnp.bfloat16)
    chan_weight = jnp.repeat(loss_table.astype(jnp.float32) / 4.0, D // GROUPS)
    diff = mixed.astype(jnp.float32) - targets.reshape(count, D).astype(jnp.float32)
    weighted = chan_weight[None, :] * diff
    loss = jnp.sum(weighted * diff) / (count * D)
    d_mixed = weighted.astype(jnp.bfloat16)
    d_attended = jnp.dot(d_mixed, jnp.transpose(w_out), preferred_element_type=jnp.float32).astype(jnp.bfloat16).reshape(shape_heads)
    d_band = d_attended[..., :half, :].reshape(row_shape)
    d_window = d_attended[..., half:, :]
    band_dq, band_dk, band_dv = lax.map(lambda group: band_backward(group[0], group[1], group[2], group[3], group[4], scale), (band_q, band_k, band_v, band_out, d_band))
    d_window_wide = d_window.astype(jnp.float32)
    d_probs = jnp.stack([jnp.einsum('lrchd,mrchd->lrchm', d_window_wide, value_pad[:, shift_row:shift_row + ROWS]) for shift_row in range(span)], axis=-1)
    delta = lax.optimization_barrier(jnp.sum(d_window_wide * window_out.astype(jnp.float32), axis=-1))[..., None, None]
    d_scores = (window_probs * (d_probs - delta) * scale).astype(jnp.bfloat16).astype(jnp.float32)
    dq_sum = jnp.zeros(window_q.shape, jnp.float32)
    dk_pad = jnp.zeros(key_pad.shape, jnp.float32)
    dv_pad = jnp.zeros(value_pad.shape, jnp.float32)
    for shift_row in range(span):
        dq_sum = dq_sum + jnp.einsum('lrchm,mrchd->lrchd', d_scores[..., shift_row], key_pad[:, shift_row:shift_row + ROWS])
        dk_pad = dk_pad.at[:, shift_row:shift_row + ROWS].add(jnp.einsum('lrchm,lrchd->mrchd', d_scores[..., shift_row], query_wide))
        dv_pad = dv_pad.at[:, shift_row:shift_row + ROWS].add(jnp.einsum('lrchm,lrchd->mrchd', window_weights[..., shift_row], d_window_wide))
    window_dq = dq_sum.astype(jnp.bfloat16)
    window_dk = dk_pad[:, REACH:REACH + ROWS].astype(jnp.bfloat16)
    window_dv = dv_pad[:, REACH:REACH + ROWS].astype(jnp.bfloat16)
    band_shape = (LEVELS, ROWS, COLS, half, head_dim)
    d_queries = jnp.concatenate([band_dq.reshape(band_shape), window_dq], axis=3).reshape(count, D)
    d_keys = jnp.concatenate([band_dk.reshape(band_shape), window_dk], axis=3).reshape(count, D)
    d_values = jnp.concatenate([band_dv.reshape(band_shape), window_dv], axis=3).reshape(count, D)
    grad = d_mixed.astype(jnp.float32)
    grad = grad + jnp.dot(d_queries, jnp.transpose(w_query), preferred_element_type=jnp.float32)
    grad = grad + jnp.dot(d_keys, jnp.transpose(w_key), preferred_element_type=jnp.float32)
    grad = grad + jnp.dot(d_values, jnp.transpose(w_value), preferred_element_type=jnp.float32)
    full_shape = (LEVELS, ROWS, COLS, D)
    return (mixed.reshape(full_shape), grad.reshape(full_shape), loss)
```

```python
import functools
import math

import jax
import jax.numpy as jnp
from jax import lax
from jax.experimental import pallas as pl
from jax.experimental.pallas import tpu as pltpu
from jax.sharding import PartitionSpec as P

HEADS = 16
HALF = 8
HD = 64
LEVELS = 3
N_LON = 16
N_LAT = 8
TOK = 192
WIDTH = 1024
BAND = 512
SCALE = 0.125
LOG2E = math.log2(math.e)
NEG = -1e30
BF = jnp.bfloat16
F32 = jnp.float32
VMEM = 40 * 1024 * 1024


def call(kernel, out_shape, flops, nbytes, **kw):
    return pl.pallas_call(
        kernel,
        out_shape=out_shape,
        compiler_params=pltpu.CompilerParams(vmem_limit_bytes=VMEM),
        cost_estimate=pl.CostEstimate(flops=flops, bytes_accessed=nbytes, transcendentals=0),
        **kw,
    )


def dot(a, b):
    return jnp.dot(a, b, preferred_element_type=F32)


def dot_nt(a, b):
    return lax.dot_general(a, b, (((1,), (1,)), ((), ())), preferred_element_type=F32)


def tr(x):
    return jnp.transpose(x)


def band_proj_kernel(tok_ref, wq_ref, wk_ref, wv_ref, out_ref):
    tok = tok_ref[...]
    q = dot(tok, wq_ref[...]).astype(BF)
    k = dot(tok, wk_ref[...]).astype(BF)
    v = dot(tok, wv_ref[...]).astype(BF)
    for hh in range(4):
        lanes = slice(64 * hh, 64 * hh + 64)
        qk = jnp.concatenate([q[:, lanes], k[:, lanes]], axis=1)
        vh = v[:, lanes]
        for l in range(LEVELS):
            for r in range(2):
                base = l * 64 + r * 32
                out_ref[2 * hh + r, 48 * l : 48 * l + 32, :] = qk[base : base + 32]
                out_ref[2 * hh + r, 48 * l + 32 : 48 * l + 48, :] = jnp.concatenate(
                    [vh[base : base + 16], vh[base + 16 : base + 32]], axis=1
                )


def band_proj(tok, wq, wk, wv):
    wspec = pl.BlockSpec((WIDTH, 256), lambda g: (0, g))
    return call(
        band_proj_kernel,
        jax.ShapeDtypeStruct((N_LON, 144, 128), BF),
        6 * TOK * WIDTH * BAND,
        4 * 1024 * 1024,
        grid=(2,),
        in_specs=[pl.BlockSpec((TOK, WIDTH), lambda g: (0, 0)), wspec, wspec, wspec],
        out_specs=pl.BlockSpec((8, 144, 128), lambda g: (g, 0, 0)),
    )(tok, wq, wk, wv)


def unpack_qkv(x):
    qk = x[:, 0:32, :].reshape(512, 128)
    v = x[:, 32:48, :]
    v = jnp.concatenate([v[:, :, 0:64], v[:, :, 64:128]], axis=1).reshape(512, 64)
    return qk[:, 0:64], qk[:, 64:128], v


def unpack_one(x):
    return jnp.concatenate([x[:, :, 0:64], x[:, :, 64:128]], axis=1).reshape(512, 64)


def pack_one(x):
    x = x.reshape(N_LON, 32, 64)
    return jnp.concatenate([x[:, 0:16, :], x[:, 16:32, :]], axis=2)


def band_fwd_kernel(x_ref, o_ref, stat_ref):
    q, k, v = unpack_qkv(x_ref[...])
    s = dot_nt(k, q) * (SCALE * LOG2E)
    top = jnp.max(s, axis=0, keepdims=True)
    e = jnp.exp2(s - top)
    rtot = 1.0 / jnp.sum(e, axis=0, keepdims=True)
    w = (e * rtot).astype(BF)
    o = tr(dot(tr(v), w)).astype(BF)
    o_ref[...] = pack_one(o)
    stat_ref[0, 0:1, :] = top
    stat_ref[0, 1:2, :] = rtot


def band_fwd(x):
    return call(
        band_fwd_kernel,
        (
            jax.ShapeDtypeStruct((N_LON, 48, 128), BF),
            jax.ShapeDtypeStruct((LEVELS, 2, 512), F32),
        ),
        12 * 512 * 512 * 64,
        1024 * 1024,
        grid=(LEVELS,),
        in_specs=[pl.BlockSpec((N_LON, 48, 128), lambda l: (0, l, 0))],
        out_specs=(
            pl.BlockSpec((N_LON, 16, 128), lambda l: (0, l, 0)),
            pl.BlockSpec((1, 2, 512), lambda l: (l, 0, 0)),
        ),
    )(x)


def band_bwd_kernel(x_ref, o_ref, stat_ref, do_ref, loss_ref, out_ref, tot_ref):
    q, k, v = unpack_qkv(x_ref[...])
    o = unpack_one(o_ref[...])
    do = unpack_one(do_ref[...])
    s = dot_nt(k, q) * (SCALE * LOG2E)
    p = jnp.exp2(s - stat_ref[0, 0:1, :]) * stat_ref[0, 1:2, :]
    w = p.astype(BF)
    dp = dot_nt(v, do)
    delta = jnp.sum(tr(do.astype(F32) * o.astype(F32)), axis=0, keepdims=True)
    ds = (p * (dp - delta) * SCALE).astype(BF)
    dv = dot(w, do).astype(BF)
    dk = dot(ds, q).astype(BF)
    dq = tr(dot(tr(k), ds)).astype(BF)
    out_ref[:, 0:32, :] = jnp.concatenate([dq, dk], axis=1).reshape(N_LON, 32, 128)
    out_ref[:, 32:48, :] = pack_one(dv)
    tot_ref[...] = jnp.broadcast_to(jnp.sum(loss_ref[:, 0, 0:128].astype(F32)), (8, 128))


def band_bwd(x, o, stat, do):
    return call(
        band_bwd_kernel,
        (
            jax.ShapeDtypeStruct((N_LON, 144, 128), BF),
            jax.ShapeDtypeStruct((8, 128), F32),
        ),
        30 * 512 * 512 * 64,
        2 * 1024 * 1024,
        grid=(LEVELS,),
        in_specs=[
            pl.BlockSpec((N_LON, 48, 128), lambda l: (0, l, 0)),
            pl.BlockSpec((N_LON, 16, 128), lambda l: (0, l, 0)),
            pl.BlockSpec((1, 2, 512), lambda l: (l, 0, 0)),
            pl.BlockSpec((N_LON, 16, 128), lambda l: (0, l, 0)),
            pl.BlockSpec((N_LON, 16, 128), lambda l: (0, 3, 0)),
        ],
        out_specs=(
            pl.BlockSpec((N_LON, 48, 128), lambda l: (0, l, 0)),
            pl.BlockSpec((8, 128), lambda l: (0, 0)),
        ),
    )(x, o, stat, do, do)


def to_halves(x):
    return jnp.concatenate(
        [x[32 * i + 16 * s : 32 * i + 16 * s + 16] for s in range(2) for i in range(6)], axis=0
    )


def from_halves(x):
    return jnp.concatenate(
        [x[96 * s + 16 * i : 96 * s + 16 * i + 16] for i in range(6) for s in range(2)], axis=0
    )


def win_proj_kernel(tok_ref, wq_ref, wk_ref, wv_ref, q_ref, k_ref, v_ref):
    tok = to_halves(tok_ref[...])
    q_ref[...] = dot(tok, wq_ref[...]).astype(BF)
    k_ref[...] = dot(tok, wk_ref[...]).astype(BF)
    v_ref[...] = dot(tok, wv_ref[...]).astype(BF)


def win_proj(tok, wq, wk, wv):
    wspec = pl.BlockSpec((WIDTH, 256), lambda g: (0, 2 + g))
    ospec = pl.BlockSpec((TOK, 256), lambda g: (0, g))
    shape = jax.ShapeDtypeStruct((TOK, BAND), BF)
    return call(
        win_proj_kernel,
        (shape, shape, shape),
        6 * TOK * WIDTH * BAND,
        4 * 1024 * 1024,
        grid=(2,),
        in_specs=[pl.BlockSpec((TOK, WIDTH), lambda g: (0, 0)), wspec, wspec, wspec],
        out_specs=(ospec, ospec, ospec),
    )(tok, wq, wk, wv)


def halo_proj_kernel(prev_ref, next_ref, wk_ref, wv_ref, k_ref, v_ref):
    tok = jnp.concatenate([to_halves(prev_ref[...]), to_halves(next_ref[...])], axis=0)
    k_ref[...] = dot(tok, wk_ref[...]).astype(BF)
    v_ref[...] = dot(tok, wv_ref[...]).astype(BF)


def halo_proj(prev, nxt, wk, wv):
    tspec = pl.BlockSpec((TOK, WIDTH), lambda g: (0, 0))
    wspec = pl.BlockSpec((WIDTH, 256), lambda g: (0, 2 + g))
    ospec = pl.BlockSpec((2 * TOK, 256), lambda g: (0, g))
    shape = jax.ShapeDtypeStruct((2 * TOK, BAND), BF)
    return call(
        halo_proj_kernel,
        (shape, shape),
        8 * TOK * WIDTH * BAND,
        3 * 1024 * 1024,
        grid=(2,),
        in_specs=[tspec, tspec, wspec, wspec],
        out_specs=(ospec, ospec),
    )(prev, nxt, wk, wv)


def window_distance(pos):
    key = lax.broadcasted_iota(jnp.int32, (288, 96), 0)
    query = lax.broadcasted_iota(jnp.int32, (288, 96), 1)
    block = (key >= 96).astype(jnp.int32) + (key >= 192).astype(jnp.int32)
    inner = key - 96 * block
    shift = jnp.where(block == 1, -2, jnp.where(block == 2, 2, 0))
    offset = shift + ((inner >> 4) & 1) - ((query >> 4) & 1)
    allowed = (inner & 15) == (query & 15)
    allowed = allowed & ((block != 1) | (pos > 0)) & ((block != 2) | (pos < N_LAT - 1))
    return jnp.where(allowed, jnp.abs(offset), 99)


def extended(own, halo, half):
    rows = slice(96 * half, 96 * half + 96)
    nrows = slice(TOK + 96 * half, TOK + 96 * half + 96)
    return jnp.concatenate([own[rows], halo[rows], halo[nrows]], axis=0)


def win_fwd_kernel(pos_ref, reach_ref, q_ref, k_ref, v_ref, hk_ref, hv_ref, o_ref, ot_ref, stat_ref):
    dist = window_distance(pos_ref[0])
    for half in range(2):
        rows = slice(96 * half, 96 * half + 96)
        q = q_ref[rows]
        k = extended(k_ref[...], hk_ref[...], half)
        vt = tr(extended(v_ref[...], hv_ref[...], half))
        outs = []
        for h in range(HALF):
            lanes = slice(64 * h, 64 * h + 64)
            s = dot_nt(k[:, lanes], q[:, lanes]) * (SCALE * LOG2E)
            s = jnp.where(dist <= reach_ref[h], s, NEG)
            top = jnp.max(s, axis=0, keepdims=True)
            e = jnp.exp2(s - top)
            rtot = 1.0 / jnp.sum(e, axis=0, keepdims=True)
            w = (e * rtot).astype(BF)
            ot = dot(vt[lanes], w)
            outs.append(ot)
            stat_ref[half, 2 * h : 2 * h + 1, :] = top
            stat_ref[half, 2 * h + 1 : 2 * h + 2, :] = rtot
        ot = jnp.concatenate(outs, axis=0)
        ot_ref[half] = ot.astype(BF)
        o_ref[rows] = tr(ot).astype(BF)


SMEM = pl.BlockSpec(memory_space=pltpu.SMEM)


def win_fwd(pos, reach, q, k, v, hk, hv):
    return call(
        win_fwd_kernel,
        (
            jax.ShapeDtypeStruct((TOK, BAND), BF),
            jax.ShapeDtypeStruct((2, BAND, 96), BF),
            jax.ShapeDtypeStruct((2, 16, 96), F32),
        ),
        64 * 288 * 128 * 64,
        2 * 1024 * 1024,
        in_specs=[SMEM, SMEM] + [pl.BlockSpec(memory_space=pltpu.VMEM)] * 5,
        out_specs=(pl.BlockSpec(memory_space=pltpu.VMEM),) * 3,
    )(pos, reach, q, k, v, hk, hv)


def win_bwd_kernel(
    pos_ref, reach_ref, q_ref, k_ref, v_ref, hk_ref, hv_ref, ot_ref, stat_ref, do_ref,
    dq_ref, own_ref, prev_ref, next_ref,
):
    dist = window_distance(pos_ref[0])
    do_all = to_halves(do_ref[...])
    for half in range(2):
        rows = slice(96 * half, 96 * half + 96)
        q = q_ref[rows]
        k = extended(k_ref[...], hk_ref[...], half)
        v = extended(v_ref[...], hv_ref[...], half)
        kt = tr(k)
        do = do_all[rows]
        dot_t = tr(do)
        ot = ot_ref[half]
        dqs = []
        for pair in range(HALF // 2):
            dks = []
            dvs = []
            for h in (2 * pair, 2 * pair + 1):
                lanes = slice(64 * h, 64 * h + 64)
                s = dot_nt(k[:, lanes], q[:, lanes]) * (SCALE * LOG2E)
                e = jnp.exp2(s - stat_ref[half, 2 * h : 2 * h + 1, :])
                p = jnp.where(dist <= reach_ref[h], e, 0.0) * stat_ref[half, 2 * h + 1 : 2 * h + 2, :]
                w = p.astype(BF)
                dp = dot_nt(v[:, lanes], do[:, lanes])
                delta = jnp.sum(
                    dot_t[lanes].astype(F32) * ot[lanes].astype(F32), axis=0, keepdims=True
                )
                ds = (p * (dp - delta) * SCALE).astype(BF)
                dvs.append(dot(w, do[:, lanes]))
                dks.append(dot(ds, q[:, lanes]))
                dqs.append(dot(kt[lanes], ds))
            out = slice(128 * pair, 128 * pair + 128)
            for n, parts in enumerate((dks, dvs)):
                both = jnp.concatenate(parts, axis=1)
                own_ref[n, rows, out] = both[0:96]
                prev_ref[n, rows, out] = both[96:192].astype(BF)
                next_ref[n, rows, out] = both[192:288].astype(BF)
        dq_ref[rows] = tr(jnp.concatenate(dqs, axis=0)).astype(BF)


def win_bwd(pos, reach, q, k, v, hk, hv, ot, stat, do):
    rim = jax.ShapeDtypeStruct((2, TOK, BAND), BF)
    return call(
        win_bwd_kernel,
        (
            jax.ShapeDtypeStruct((TOK, BAND), BF),
            jax.ShapeDtypeStruct((2, TOK, BAND), F32),
            rim,
            rim,
        ),
        160 * 288 * 128 * 64,
        4 * 1024 * 1024,
        in_specs=[SMEM, SMEM] + [pl.BlockSpec(memory_space=pltpu.VMEM)] * 8,
        out_specs=(pl.BlockSpec(memory_space=pltpu.VMEM),) * 4,
    )(pos, reach, q, k, v, hk, hv, ot, stat, do)


def mid_kernel(table_ref, tok_ref, tgt_ref, o_ref, win_ref, wo_ref, mixed_ref, dm_ref, send_ref, dwin_ref):
    cols = []
    for pair in range(HALF // 2):
        parts = []
        for l in range(LEVELS):
            for r in range(2):
                a = o_ref[4 * pair + r, 16 * l : 16 * l + 16, :]
                b = o_ref[4 * pair + 2 + r, 16 * l : 16 * l + 16, :]
                parts.append(jnp.concatenate([a[:, 0:64], b[:, 0:64]], axis=1))
                parts.append(jnp.concatenate([a[:, 64:128], b[:, 64:128]], axis=1))
        cols.append(jnp.concatenate(parts, axis=0))
    att = jnp.concatenate(cols + [from_halves(win_ref[...])], axis=1)
    mixed = (tok_ref[...].astype(F32) + dot(att, wo_ref[...])).astype(BF)
    mixed_ref[...] = mixed
    lane = lax.broadcasted_iota(jnp.int32, (1, WIDTH), 1)
    weight = jnp.zeros((1, WIDTH), F32)
    for g in range(4):
        here = (lane >= 256 * g) & (lane < 256 * g + 256)
        weight = jnp.where(here, table_ref[g].astype(F32) * 0.25, weight)
    diff = mixed.astype(F32) - tgt_ref[...].astype(F32)
    weighted = weight * diff
    total = jnp.sum(weighted * diff)
    dm = weighted.astype(BF)
    dm_ref[...] = dm
    d_att = dot_nt(dm, wo_ref[...]).astype(BF)
    dwin_ref[...] = d_att[:, BAND:]
    for h in range(HALF):
        dh = d_att[:, 64 * h : 64 * h + 64]
        for l in range(LEVELS):
            for r in range(2):
                base = 64 * l + 32 * r
                send_ref[2 * h + r, 16 * l : 16 * l + 16, :] = jnp.concatenate(
                    [dh[base : base + 16], dh[base + 16 : base + 32]], axis=1
                )
    total = jnp.broadcast_to(total, (16, 128))
    high = total.astype(BF).astype(F32)
    mid = (total - high).astype(BF).astype(F32)
    low = total - high - mid
    at = lax.broadcasted_iota(jnp.int32, (16, 128), 1)
    parts = jnp.where(at == 0, high, jnp.where(at == 1, mid, jnp.where(at == 2, low, 0.0)))
    parts = parts.astype(BF)
    for j in range(N_LON):
        send_ref[j, 48:64, :] = parts


def mid(table, tok, tgt, o, win, wo):
    return call(
        mid_kernel,
        (
            jax.ShapeDtypeStruct((TOK, WIDTH), BF),
            jax.ShapeDtypeStruct((TOK, WIDTH), BF),
            jax.ShapeDtypeStruct((N_LON, 64, 128), BF),
            jax.ShapeDtypeStruct((TOK, BAND), BF),
        ),
        4 * TOK * WIDTH * WIDTH,
        4 * 1024 * 1024,
        in_specs=[SMEM] + [pl.BlockSpec(memory_space=pltpu.VMEM)] * 5,
        out_specs=(pl.BlockSpec(memory_space=pltpu.VMEM),) * 4,
    )(table, tok, tgt, o, win, wo)


def win_grad_kernel(dm_ref, dq_ref, own_ref, fp_ref, fn_ref, wq_ref, wk_ref, wv_ref, out_ref):
    dq = dq_ref[...]
    dk = (own_ref[0] + fp_ref[0].astype(F32) + fn_ref[0].astype(F32)).astype(BF)
    dv = (own_ref[1] + fp_ref[1].astype(F32) + fn_ref[1].astype(F32)).astype(BF)
    g = dot_nt(dq, wq_ref[...]) + dot_nt(dk, wk_ref[...]) + dot_nt(dv, wv_ref[...])
    out_ref[...] = dm_ref[...].astype(F32) + from_halves(g)


def win_grad(dm, dq, own, fp, fn, wq, wk, wv):
    wspec = pl.BlockSpec((256, BAND), lambda g: (g, 1))
    whole3 = pl.BlockSpec((2, TOK, BAND), lambda g: (0, 0, 0))
    nspec = pl.BlockSpec((TOK, 256), lambda g: (0, g))
    return call(
        win_grad_kernel,
        jax.ShapeDtypeStruct((TOK, WIDTH), F32),
        6 * TOK * WIDTH * BAND,
        5 * 1024 * 1024,
        grid=(4,),
        in_specs=[nspec, pl.BlockSpec((TOK, BAND), lambda g: (0, 0)), whole3, whole3, whole3]
        + [wspec] * 3,
        out_specs=nspec,
    )(dm, dq, own, fp, fn, wq, wk, wv)


def band_grad_kernel(x_ref, base_ref, wq_ref, wk_ref, wv_ref, out_ref, dq_s, dk_s, dv_s):
    @pl.when(pl.program_id(0) == 0)
    def _():
        for pair in range(HALF // 2):
            lanes = slice(128 * pair, 128 * pair + 128)
            for l in range(LEVELS):
                for r in range(2):
                    base = 64 * l + 32 * r
                    a = x_ref[4 * pair + r, 48 * l : 48 * l + 48, :]
                    b = x_ref[4 * pair + 2 + r, 48 * l : 48 * l + 48, :]
                    first = jnp.concatenate([a[:, 0:64], b[:, 0:64]], axis=1)
                    second = jnp.concatenate([a[:, 64:128], b[:, 64:128]], axis=1)
                    dq_s[base : base + 32, lanes] = first[0:32]
                    dk_s[base : base + 32, lanes] = second[0:32]
                    dv_s[base : base + 16, lanes] = first[32:48]
                    dv_s[base + 16 : base + 32, lanes] = second[32:48]

    g = dot_nt(dq_s[...], wq_ref[...]) + dot_nt(dk_s[...], wk_ref[...])
    out_ref[...] = base_ref[...] + g + dot_nt(dv_s[...], wv_ref[...])


def band_grad(x, base, wq, wk, wv):
    wspec = pl.BlockSpec((256, BAND), lambda g: (g, 0))
    nspec = pl.BlockSpec((TOK, 256), lambda g: (0, g))
    return call(
        band_grad_kernel,
        jax.ShapeDtypeStruct((TOK, WIDTH), F32),
        6 * TOK * WIDTH * BAND,
        5 * 1024 * 1024,
        grid=(4,),
        in_specs=[pl.BlockSpec((N_LON, 144, 128), lambda g: (0, 0, 0)), nspec] + [wspec] * 3,
        out_specs=nspec,
        scratch_shapes=[pltpu.VMEM((TOK, BAND), BF)] * 3,
    )(x, base, wq, wk, wv)


def swap(x):
    return lax.all_to_all(x, "lon", 0, 0, tiled=True)


UP = [(i, (i + 1) % N_LAT) for i in range(N_LAT)]
DOWN = [((i + 1) % N_LAT, i) for i in range(N_LAT)]


def per_device(tokens, targets, w_query, w_key, w_value, w_out, window_reach, loss_table):
    levels, rows, cols, width = tokens.shape
    count = levels * rows * cols
    tok = tokens.reshape(count, width)
    tgt = targets.reshape(count, width)
    pos = lax.axis_index("lat").astype(jnp.int32).reshape(1)

    with jax.named_scope("band_projection"):
        sent = band_proj(tok, w_query, w_key, w_value)
    with jax.named_scope("halo_tokens"):
        prev = lax.ppermute(tok, "lat", UP)
        nxt = lax.ppermute(tok, "lat", DOWN)
    with jax.named_scope("band_qkv_exchange"):
        x = swap(sent)
    with jax.named_scope("window_projection"):
        q, k, v = win_proj(tok, w_query, w_key, w_value)
        hk, hv = halo_proj(prev, nxt, w_key, w_value)
    with jax.named_scope("band_forward"):
        o, stat = band_fwd(x)
        o_back = swap(o)
    with jax.named_scope("window_forward"):
        win, ot, wstat = win_fwd(pos, window_reach, q, k, v, hk, hv)
    with jax.named_scope("middle"):
        mixed, dm, dsend, dwin = mid(loss_table, tok, tgt, o_back, win, w_out)
        do = swap(dsend)
    with jax.named_scope("window_backward"):
        dqw, own, rim_prev, rim_next = win_bwd(
            pos, window_reach, q, k, v, hk, hv, ot, wstat, dwin
        )
        from_prev = lax.ppermute(rim_next, "lat", UP)
        from_next = lax.ppermute(rim_prev, "lat", DOWN)
    with jax.named_scope("band_backward"):
        dsent, total = band_bwd(x, o, stat, do)
        dx = swap(dsent)
    with jax.named_scope("loss_sum"):
        for step in (1, 2, 4):
            total = total + lax.ppermute(total, "lat", [(i, i ^ step) for i in range(N_LAT)])
        loss = total[0, 0] / (count * width * N_LON * N_LAT)
    with jax.named_scope("token_gradient"):
        base = win_grad(dm, dqw, own, from_prev, from_next, w_query, w_key, w_value)
        grad = band_grad(dx, base, w_query, w_key, w_value)
    full = (levels, rows, cols, width)
    return (mixed.reshape(full), grad.reshape(full), loss)


def solution(mesh):
    spec = P(None, "lat", "lon", None)
    return jax.shard_map(
        per_device,
        mesh=mesh,
        in_specs=(spec, spec, P(), P(), P(), P(), P(), P()),
        out_specs=(spec, spec, P()),
        check_vma=False,
    )
```

```python
import functools
import math

import jax
import jax.numpy as jnp
from jax import lax
from jax.experimental import pallas as pl
from jax.experimental.pallas import tpu as pltpu
from jax.sharding import PartitionSpec as P

HEADS = 16
HALF = 8
HD = 64
LEVELS = 3
N_LON = 16
N_LAT = 8
TOK = 192
WIDTH = 1024
BAND = 512
SCALE = 0.125
LOG2E = math.log2(math.e)
NEG = -1e30
BF = jnp.bfloat16
F32 = jnp.float32
VMEM = 32 * 1024 * 1024


def call(kernel, outs, flops, nbytes, ins, scratch=()):
    return pl.pallas_call(
        kernel,
        grid=(1,),
        in_specs=[spec for spec, _ in ins],
        out_specs=tuple(spec for spec, _ in outs),
        out_shape=tuple(shape for _, shape in outs),
        scratch_shapes=list(scratch),
        compiler_params=pltpu.CompilerParams(vmem_limit_bytes=VMEM),
        cost_estimate=pl.CostEstimate(flops=50 * flops, bytes_accessed=nbytes, transcendentals=0),
    )(*[x for _, x in ins])


def in_smem(x):
    return (pl.BlockSpec(memory_space=pltpu.SMEM), x)


def in_vmem(x):
    return (pl.BlockSpec(memory_space=pltpu.VMEM), x)


def in_hbm(x):
    return (pl.BlockSpec(memory_space=pltpu.HBM), hbm(x))


def out_vmem(shape, dtype):
    return (pl.BlockSpec(memory_space=pltpu.VMEM), pltpu.VMEM(shape, dtype))


def out_hbm(shape, dtype):
    return (pl.BlockSpec(memory_space=pltpu.HBM), jax.ShapeDtypeStruct(shape, dtype))


def out_block(shape, dtype):
    zeros = (0,) * len(shape)
    return (pl.BlockSpec(shape, lambda g: zeros), jax.ShapeDtypeStruct(shape, dtype))


def begin(pairs, sems):
    copies = [pltpu.make_async_copy(a, b, sems.at[n]) for n, (a, b) in enumerate(pairs)]
    for copy in copies:
        copy.start()
    return copies


def hbm(x):
    return pltpu.with_memory_space_constraint(x, pltpu.HBM)


def dot(a, b):
    return jnp.dot(a, b, preferred_element_type=F32)


def dot_nt(a, b):
    return lax.dot_general(a, b, (((1,), (1,)), ((), ())), preferred_element_type=F32)


def tr(x):
    return jnp.transpose(x)


def band_proj_kernel(
    tok_hbm, wq_hbm, wk_hbm, wv_hbm, out_ref, tok_ref, wq_ref, wk_ref, wv_ref, sems
):
    lanes = pl.ds(0, BAND)
    copies = begin(
        [
            (tok_hbm, tok_ref),
            (wq_hbm.at[:, lanes], wq_ref),
            (wk_hbm.at[:, lanes], wk_ref),
            (wv_hbm.at[:, lanes], wv_ref),
        ],
        sems,
    )
    copies[0].wait()
    tok = tok_ref[...]
    copies[1].wait()
    q = dot(tok, wq_ref[...]).astype(BF)
    copies[2].wait()
    k = dot(tok, wk_ref[...]).astype(BF)
    copies[3].wait()
    v = dot(tok, wv_ref[...]).astype(BF)
    for h in range(HALF):
        lanes = slice(64 * h, 64 * h + 64)
        qk = jnp.concatenate([q[:, lanes], k[:, lanes]], axis=1)
        vh = v[:, lanes]
        for l in range(LEVELS):
            for r in range(2):
                base = l * 64 + r * 32
                out_ref[2 * h + r, 48 * l : 48 * l + 32, :] = qk[base : base + 32]
                out_ref[2 * h + r, 48 * l + 32 : 48 * l + 48, :] = jnp.concatenate(
                    [vh[base : base + 16], vh[base + 16 : base + 32]], axis=1
                )


WEIGHT_HALF = pltpu.VMEM((WIDTH, BAND), BF)


def band_proj(tok, wq, wk, wv):
    return call(
        band_proj_kernel,
        [out_block((N_LON, 144, 128), BF)],
        6 * TOK * WIDTH * BAND,
        4 * 1024 * 1024,
        [in_hbm(x) for x in (tok, wq, wk, wv)],
        [pltpu.VMEM((TOK, WIDTH), BF)] + [WEIGHT_HALF] * 3 + [pltpu.SemaphoreType.DMA((4,))],
    )[0]


def unpack_qkv(x):
    qk = x[:, 0:32, :].reshape(512, 128)
    v = x[:, 32:48, :]
    v = jnp.concatenate([v[:, :, 0:64], v[:, :, 64:128]], axis=1).reshape(512, 64)
    return qk[:, 0:64], qk[:, 64:128], v


def unpack_one(x):
    return jnp.concatenate([x[:, :, 0:64], x[:, :, 64:128]], axis=1).reshape(512, 64)


def pack_one(x):
    x = x.reshape(N_LON, 32, 64)
    return jnp.concatenate([x[:, 0:16, :], x[:, 16:32, :]], axis=2)


def band_fwd_kernel(x_ref, o_ref, stat_ref):
    for l in range(LEVELS):
        q, k, v = unpack_qkv(x_ref[:, 48 * l : 48 * l + 48, :])
        s = dot_nt(k, q) * (SCALE * LOG2E)
        top = jnp.max(s, axis=0, keepdims=True)
        e = jnp.exp2(s - top)
        rtot = 1.0 / jnp.sum(e, axis=0, keepdims=True)
        w = (e * rtot).astype(BF)
        o = tr(dot(tr(v), w)).astype(BF)
        o_ref[:, 16 * l : 16 * l + 16, :] = pack_one(o)
        stat_ref[l, 0:1, :] = top
        stat_ref[l, 1:2, :] = rtot


def band_fwd(x):
    return call(
        band_fwd_kernel,
        [out_block((N_LON, 48, 128), BF), out_vmem((LEVELS, 2, 512), F32)],
        12 * 512 * 512 * 64,
        1024 * 1024,
        [in_vmem(x)],
    )


def band_bwd_kernel(x_ref, o_ref, stat_ref, do_ref, mine_ref, other_ref, out_ref):
    total = jnp.broadcast_to(mine_ref[0:1, :] + other_ref[0:1, :], (16, 128))
    high = total.astype(BF).astype(F32)
    mid = (total - high).astype(BF).astype(F32)
    low = total - high - mid
    at = lax.broadcasted_iota(jnp.int32, (16, 128), 1)
    parts = jnp.where(at == 0, high, jnp.where(at == 1, mid, jnp.where(at == 2, low, 0.0)))
    parts = parts.astype(BF)
    for j in range(N_LON):
        out_ref[j, 144:160, :] = parts
    for l in range(LEVELS):
        q, k, v = unpack_qkv(x_ref[:, 48 * l : 48 * l + 48, :])
        o = unpack_one(o_ref[:, 16 * l : 16 * l + 16, :])
        do = unpack_one(do_ref[:, 16 * l : 16 * l + 16, :])
        s = dot_nt(k, q) * (SCALE * LOG2E)
        p = jnp.exp2(s - stat_ref[l, 0:1, :]) * stat_ref[l, 1:2, :]
        w = p.astype(BF)
        dp = dot_nt(v, do)
        delta = jnp.sum(tr(do.astype(F32) * o.astype(F32)), axis=0, keepdims=True)
        ds = (p * (dp - delta) * SCALE).astype(BF)
        dv = dot(w, do).astype(BF)
        dk = dot(ds, q).astype(BF)
        dq = tr(dot(tr(k), ds)).astype(BF)
        out_ref[:, 48 * l : 48 * l + 32, :] = jnp.concatenate([dq, dk], axis=1).reshape(
            N_LON, 32, 128
        )
        out_ref[:, 48 * l + 32 : 48 * l + 48, :] = pack_one(dv)


def band_bwd(x, o, stat, do, mine, other):
    return call(
        band_bwd_kernel,
        [out_block((N_LON, 160, 128), BF)],
        30 * 512 * 512 * 64,
        2 * 1024 * 1024,
        [in_vmem(y) for y in (x, o, stat, do, mine, other)],
    )[0]


def to_halves(x):
    return jnp.concatenate(
        [x[32 * i + 16 * s : 32 * i + 16 * s + 16] for s in range(2) for i in range(6)], axis=0
    )


def from_halves(x):
    return jnp.concatenate(
        [x[96 * s + 16 * i : 96 * s + 16 * i + 16] for i in range(6) for s in range(2)], axis=0
    )


def win_proj_kernel(
    tok_hbm, wq_hbm, wk_hbm, wv_hbm, q_ref, k_ref, v_ref, tok_ref, wq_ref, wk_ref, wv_ref, sems
):
    lanes = pl.ds(BAND, BAND)
    copies = begin(
        [
            (tok_hbm, tok_ref),
            (wq_hbm.at[:, lanes], wq_ref),
            (wk_hbm.at[:, lanes], wk_ref),
            (wv_hbm.at[:, lanes], wv_ref),
        ],
        sems,
    )
    copies[0].wait()
    tok = to_halves(tok_ref[...])
    copies[1].wait()
    q_ref[...] = dot(tok, wq_ref[...]).astype(BF)
    copies[2].wait()
    k_ref[...] = dot(tok, wk_ref[...]).astype(BF)
    copies[3].wait()
    v_ref[...] = dot(tok, wv_ref[...]).astype(BF)


def win_proj(tok, wq, wk, wv):
    return call(
        win_proj_kernel,
        [out_vmem((TOK, BAND), BF)] * 3,
        6 * TOK * WIDTH * BAND,
        4 * 1024 * 1024,
        [in_hbm(x) for x in (tok, wq, wk, wv)],
        [pltpu.VMEM((TOK, WIDTH), BF)] + [WEIGHT_HALF] * 3 + [pltpu.SemaphoreType.DMA((4,))],
    )


def window_distance(pos):
    key = lax.broadcasted_iota(jnp.int32, (288, 96), 0)
    query = lax.broadcasted_iota(jnp.int32, (288, 96), 1)
    block = (key >= 96).astype(jnp.int32) + (key >= 192).astype(jnp.int32)
    inner = key - 96 * block
    shift = jnp.where(block == 1, -2, jnp.where(block == 2, 2, 0))
    offset = shift + ((inner >> 4) & 1) - ((query >> 4) & 1)
    allowed = (inner & 15) == (query & 15)
    allowed = allowed & ((block != 1) | (pos > 0)) & ((block != 2) | (pos < N_LAT - 1))
    return jnp.where(allowed, jnp.abs(offset), 99)


def extended(own, halo, half):
    rows = slice(96 * half, 96 * half + 96)
    nrows = slice(TOK + 96 * half, TOK + 96 * half + 96)
    return jnp.concatenate([own[rows], halo[rows], halo[nrows]], axis=0)


def win_fwd_kernel(
    pos_ref, reach_ref, q_ref, k_ref, v_ref, prev_ref, next_ref,
    wk_hbm, wv_hbm, o_ref, ot_ref, stat_ref, hk_ref, hv_ref, wk_ref, wv_ref, sems,
):
    lanes = pl.ds(BAND, BAND)
    copies = begin([(wk_hbm.at[:, lanes], wk_ref), (wv_hbm.at[:, lanes], wv_ref)], sems)
    dist = window_distance(pos_ref[0])
    near = jnp.concatenate([to_halves(prev_ref[...]), to_halves(next_ref[...])], axis=0)
    copies[0].wait()
    hk_ref[...] = dot(near, wk_ref[...]).astype(BF)
    copies[1].wait()
    hv_ref[...] = dot(near, wv_ref[...]).astype(BF)
    for half in range(2):
        rows = slice(96 * half, 96 * half + 96)
        q = q_ref[rows]
        k = extended(k_ref[...], hk_ref[...], half)
        vt = tr(extended(v_ref[...], hv_ref[...], half))
        outs = []
        for h in range(HALF):
            lanes = slice(64 * h, 64 * h + 64)
            s = dot_nt(k[:, lanes], q[:, lanes]) * (SCALE * LOG2E)
            s = jnp.where(dist <= reach_ref[h], s, NEG)
            top = jnp.max(s, axis=0, keepdims=True)
            e = jnp.exp2(s - top)
            rtot = 1.0 / jnp.sum(e, axis=0, keepdims=True)
            w = (e * rtot).astype(BF)
            ot = dot(vt[lanes], w)
            outs.append(ot)
            stat_ref[half, 2 * h : 2 * h + 1, :] = top
            stat_ref[half, 2 * h + 1 : 2 * h + 2, :] = rtot
        ot = jnp.concatenate(outs, axis=0)
        ot_ref[half] = ot.astype(BF)
        o_ref[rows] = tr(ot).astype(BF)


def win_fwd(pos, reach, q, k, v, prev, nxt, wk, wv):
    return call(
        win_fwd_kernel,
        [
            out_vmem((TOK, BAND), BF),
            out_vmem((2, BAND, 96), BF),
            out_vmem((2, 16, 96), F32),
            out_vmem((2 * TOK, BAND), BF),
            out_vmem((2 * TOK, BAND), BF),
        ],
        64 * 288 * 128 * 64 + 8 * TOK * WIDTH * BAND,
        6 * 1024 * 1024,
        [in_smem(pos), in_smem(reach)]
        + [in_vmem(x) for x in (q, k, v, prev, nxt)]
        + [in_hbm(x) for x in (wk, wv)],
        [WEIGHT_HALF] * 2 + [pltpu.SemaphoreType.DMA((2,))],
    )


def win_bwd_kernel(
    pos_ref, reach_ref, q_ref, k_ref, v_ref, hk_ref, hv_ref, ot_ref, stat_ref, do_ref,
    p0_ref, p1_ref, p2_ref, p3_ref, dq_ref, own_ref, prev_ref, next_ref, sum_ref,
):
    sum_ref[...] = p0_ref[...] + p1_ref[...] + p2_ref[...] + p3_ref[...]
    dist = window_distance(pos_ref[0])
    do_all = to_halves(do_ref[...])
    for half in range(2):
        rows = slice(96 * half, 96 * half + 96)
        q = q_ref[rows]
        k = extended(k_ref[...], hk_ref[...], half)
        v = extended(v_ref[...], hv_ref[...], half)
        kt = tr(k)
        do = do_all[rows]
        dot_t = tr(do)
        ot = ot_ref[half]
        dqs = []
        for pair in range(HALF // 2):
            dks = []
            dvs = []
            for h in (2 * pair, 2 * pair + 1):
                lanes = slice(64 * h, 64 * h + 64)
                s = dot_nt(k[:, lanes], q[:, lanes]) * (SCALE * LOG2E)
                e = jnp.exp2(s - stat_ref[half, 2 * h : 2 * h + 1, :])
                p = jnp.where(dist <= reach_ref[h], e, 0.0) * stat_ref[half, 2 * h + 1 : 2 * h + 2, :]
                w = p.astype(BF)
                dp = dot_nt(v[:, lanes], do[:, lanes])
                delta = jnp.sum(
                    dot_t[lanes].astype(F32) * ot[lanes].astype(F32), axis=0, keepdims=True
                )
                ds = (p * (dp - delta) * SCALE).astype(BF)
                dvs.append(dot(w, do[:, lanes]))
                dks.append(dot(ds, q[:, lanes]))
                dqs.append(dot(kt[lanes], ds))
            out = slice(128 * pair, 128 * pair + 128)
            for n, parts in enumerate((dks, dvs)):
                both = jnp.concatenate(parts, axis=1)
                own_ref[n, rows, out] = both[0:96]
                prev_ref[n, rows, out] = both[96:192].astype(BF)
                next_ref[n, rows, out] = both[192:288].astype(BF)
        dq_ref[rows] = tr(jnp.concatenate(dqs, axis=0)).astype(BF)


def win_bwd(pos, reach, q, k, v, hk, hv, ot, stat, do, losses):
    return call(
        win_bwd_kernel,
        [
            out_vmem((TOK, BAND), BF),
            out_block((2, TOK, BAND), F32),
            out_block((2, TOK, BAND), BF),
            out_block((2, TOK, BAND), BF),
            out_block((8, 128), F32),
        ],
        160 * 288 * 128 * 64,
        4 * 1024 * 1024,
        [in_smem(pos), in_smem(reach)]
        + [in_vmem(x) for x in (q, k, v, hk, hv, ot, stat, do, *losses)],
    )


def mid_kernel(
    table_ref, tok_hbm, tgt_hbm, wo_hbm, o_ref, win_ref, mixed_hbm, dm_hbm, send_ref, dwin_ref, sum_ref,
    tok_ref, tgt_ref, wo_ref, mixed_ref, dm_ref, att_s, sems,
):
    copies = begin([(wo_hbm, wo_ref), (tok_hbm, tok_ref), (tgt_hbm, tgt_ref)], sems)
    for pair in range(HALF // 2):
        lanes = slice(128 * pair, 128 * pair + 128)
        for l in range(LEVELS):
            for r in range(2):
                base = 64 * l + 32 * r
                a = o_ref[4 * pair + r, 16 * l : 16 * l + 16, :]
                b = o_ref[4 * pair + 2 + r, 16 * l : 16 * l + 16, :]
                att_s[base : base + 16, lanes] = jnp.concatenate([a[:, 0:64], b[:, 0:64]], axis=1)
                att_s[base + 16 : base + 32, lanes] = jnp.concatenate(
                    [a[:, 64:128], b[:, 64:128]], axis=1
                )
    att_s[:, BAND:] = from_halves(win_ref[...])
    att = att_s[...]
    for copy in copies:
        copy.wait()
    d_att = jnp.zeros((TOK, WIDTH), F32)
    total = jnp.zeros((8, 256), F32)
    for g in range(4):
        lanes = slice(256 * g, 256 * g + 256)
        mixed = (tok_ref[:, lanes].astype(F32) + dot(att, wo_ref[:, lanes])).astype(BF)
        mixed_ref[:, lanes] = mixed
        diff = mixed.astype(F32) - tgt_ref[:, lanes].astype(F32)
        weighted = (table_ref[g].astype(F32) * 0.25) * diff
        total = total + jnp.sum((weighted * diff).reshape(TOK // 8, 8, 256), axis=0)
        dm = weighted.astype(BF)
        dm_ref[:, lanes] = dm
        d_att = d_att + dot_nt(dm, wo_ref[:, lanes])
    copies = begin([(mixed_ref, mixed_hbm), (dm_ref, dm_hbm)], sems)
    d_att = d_att.astype(BF)
    dwin_ref[...] = d_att[:, BAND:]
    for h in range(HALF):
        dh = d_att[:, 64 * h : 64 * h + 64]
        for l in range(LEVELS):
            for r in range(2):
                base = 64 * l + 32 * r
                send_ref[2 * h + r, 16 * l : 16 * l + 16, :] = jnp.concatenate(
                    [dh[base : base + 16], dh[base + 16 : base + 32]], axis=1
                )
    sum_ref[...] = jnp.broadcast_to(jnp.sum(total), (8, 128))
    for copy in copies:
        copy.wait()


def mid(table, tok, tgt, o, win, wo):
    return call(
        mid_kernel,
        [
            out_hbm((TOK, WIDTH), BF),
            out_hbm((TOK, WIDTH), BF),
            out_block((N_LON, 48, 128), BF),
            out_vmem((TOK, BAND), BF),
            out_block((8, 128), F32),
        ],
        4 * TOK * WIDTH * WIDTH,
        4 * 1024 * 1024,
        [in_smem(table)]
        + [in_hbm(x) for x in (tok, tgt, wo)]
        + [in_vmem(x) for x in (o, win)],
        [pltpu.VMEM((TOK, WIDTH), BF)] * 2
        + [pltpu.VMEM((WIDTH, WIDTH), BF)]
        + [pltpu.VMEM((TOK, WIDTH), BF)] * 3
        + [pltpu.SemaphoreType.DMA((3,))],
    )


def win_grad_kernel(
    dq_ref, dm_hbm, own_hbm, fp_hbm, fn_hbm, wq_hbm, wk_hbm, wv_hbm,
    out_ref, dm_ref, own_ref, fp_ref, fn_ref, wq_ref, wk_ref, wv_ref, sems,
):
    window = pl.ds(BAND, BAND)
    copies = begin(
        [
            (wq_hbm.at[:, window], wq_ref),
            (wk_hbm.at[:, window], wk_ref),
            (wv_hbm.at[:, window], wv_ref),
            (own_hbm, own_ref),
            (fp_hbm, fp_ref),
            (fn_hbm, fn_ref),
            (dm_hbm, dm_ref),
        ],
        sems,
    )
    dq = dq_ref[...]
    for copy in copies[3:6]:
        copy.wait()
    dk = (own_ref[0] + fp_ref[0].astype(F32) + fn_ref[0].astype(F32)).astype(BF)
    dv = (own_ref[1] + fp_ref[1].astype(F32) + fn_ref[1].astype(F32)).astype(BF)
    for copy in copies[:3]:
        copy.wait()
    g = dot_nt(dq, wq_ref[...]) + dot_nt(dk, wk_ref[...]) + dot_nt(dv, wv_ref[...])
    copies[6].wait()
    out_ref[...] = dm_ref[...].astype(F32) + from_halves(g)


def win_grad(dm, dq, own, fp, fn, wq, wk, wv):
    return call(
        win_grad_kernel,
        [out_block((TOK, WIDTH), F32)],
        6 * TOK * WIDTH * BAND,
        8 * 1024 * 1024,
        [in_vmem(dq)] + [in_hbm(x) for x in (dm, own, fp, fn, wq, wk, wv)],
        [
            pltpu.VMEM((TOK, WIDTH), BF),
            pltpu.VMEM((2, TOK, BAND), F32),
            pltpu.VMEM((2, TOK, BAND), BF),
            pltpu.VMEM((2, TOK, BAND), BF),
        ]
        + [WEIGHT_HALF] * 3
        + [pltpu.SemaphoreType.DMA((7,))],
    )[0]


def band_grad_kernel(
    x_ref, base_hbm, wq_hbm, wk_hbm, wv_hbm, out_hbm, loss_ref,
    base_ref, wq_ref, wk_ref, wv_ref, dq_s, dk_s, dv_s, out_s, sems,
):
    band = pl.ds(0, BAND)
    loads = begin(
        [
            (wq_hbm.at[:, band], wq_ref),
            (wk_hbm.at[:, band], wk_ref),
            (wv_hbm.at[:, band], wv_ref),
            (base_hbm, base_ref),
        ],
        sems,
    )
    for pair in range(HALF // 2):
        lanes = slice(128 * pair, 128 * pair + 128)
        for l in range(LEVELS):
            for r in range(2):
                base = 64 * l + 32 * r
                a = x_ref[4 * pair + r, 48 * l : 48 * l + 48, :]
                b = x_ref[4 * pair + 2 + r, 48 * l : 48 * l + 48, :]
                first = jnp.concatenate([a[:, 0:64], b[:, 0:64]], axis=1)
                second = jnp.concatenate([a[:, 64:128], b[:, 64:128]], axis=1)
                dq_s[base : base + 32, lanes] = first[0:32]
                dk_s[base : base + 32, lanes] = second[0:32]
                dv_s[base : base + 16, lanes] = first[32:48]
                dv_s[base + 16 : base + 32, lanes] = second[32:48]
    dq = dq_s[...]
    dk = dk_s[...]
    dv = dv_s[...]
    for load in loads:
        load.wait()
    copies = []
    for n in range(4):
        rows = slice(256 * n, 256 * n + 256)
        g = dot_nt(dq, wq_ref[rows, :]) + dot_nt(dk, wk_ref[rows, :])
        out_s[:, rows] = base_ref[:, rows] + g + dot_nt(dv, wv_ref[rows, :])
        lanes = pl.ds(256 * n, 256)
        copy = pltpu.make_async_copy(out_s.at[:, lanes], out_hbm.at[:, lanes], sems.at[n])
        copy.start()
        copies.append(copy)
    loss_ref[0, 0] = jnp.sum(x_ref[:, 144, :].astype(F32)) * (1.0 / 25165824)
    for copy in copies:
        copy.wait()


def band_grad(x, base, wq, wk, wv):
    return call(
        band_grad_kernel,
        [
            out_hbm((TOK, WIDTH), F32),
            (pl.BlockSpec(memory_space=pltpu.SMEM), jax.ShapeDtypeStruct((1, 1), F32)),
        ],
        6 * TOK * WIDTH * BAND,
        5 * 1024 * 1024,
        [in_vmem(x)] + [in_hbm(y) for y in (base, wq, wk, wv)],
        [pltpu.VMEM((TOK, WIDTH), F32)]
        + [WEIGHT_HALF] * 3
        + [pltpu.VMEM((TOK, BAND), BF)] * 3
        + [pltpu.VMEM((TOK, WIDTH), F32), pltpu.SemaphoreType.DMA((4,))],
    )


def swap(x):
    return lax.all_to_all(x, "lon", 0, 0, tiled=True)


UP = [(i, (i + 1) % N_LAT) for i in range(N_LAT)]
DOWN = [((i + 1) % N_LAT, i) for i in range(N_LAT)]


def per_device(tokens, targets, w_query, w_key, w_value, w_out, window_reach, loss_table):
    levels, rows, cols, width = tokens.shape
    count = levels * rows * cols
    tok = tokens.reshape(count, width)
    tgt = targets.reshape(count, width)
    pos = lax.axis_index("lat").astype(jnp.int32).reshape(1)
    with jax.named_scope("band_projection"):
        sent = band_proj(tok, w_query, w_key, w_value)
    with jax.named_scope("halo_tokens"):
        prev = lax.ppermute(tok, "lat", UP)
        nxt = lax.ppermute(tok, "lat", DOWN)
    with jax.named_scope("band_qkv_exchange"):
        x = swap(sent)
    with jax.named_scope("window_projection"):
        q, k, v = win_proj(tok, w_query, w_key, w_value)
        x, q, k, v = lax.optimization_barrier((x, q, k, v))
    with jax.named_scope("band_forward"):
        o, stat = band_fwd(x)
        o_back = swap(o)
    with jax.named_scope("window_forward"):
        win, ot, wstat, hk, hv = win_fwd(pos, window_reach, q, k, v, prev, nxt, w_key, w_value)
    with jax.named_scope("middle"):
        mixed, dm, dsend, dwin, part = mid(loss_table, tok, tgt, o_back, win, w_out)
        losses = [part] + [
            lax.ppermute(part, "lat", [(i, i ^ step) for i in range(N_LAT)]) for step in (1, 2, 3)
        ]
        do = swap(dsend)
    with jax.named_scope("window_backward"):
        dqw, own, rim_prev, rim_next, four = win_bwd(
            pos, window_reach, q, k, v, hk, hv, ot, wstat, dwin, losses
        )
        far = lax.ppermute(four, "lat", [(i, i ^ 4) for i in range(N_LAT)])
        from_prev = lax.ppermute(rim_next, "lat", UP)
        from_next = lax.ppermute(rim_prev, "lat", DOWN)
    with jax.named_scope("band_backward"):
        dsent = band_bwd(x, o, stat, do, four, far)
        dx = swap(dsent)
    with jax.named_scope("token_gradient"):
        base = win_grad(dm, dqw, own, from_prev, from_next, w_query, w_key, w_value)
        grad, loss = band_grad(dx, base, w_query, w_key, w_value)
    full = (levels, rows, cols, width)
    return (mixed.reshape(full), grad.reshape(full), loss.reshape(()))


def solution(mesh):
    spec = P(None, "lat", "lon", None)
    return jax.shard_map(
        per_device,
        mesh=mesh,
        in_specs=(spec, spec, P(), P(), P(), P(), P(), P()),
        out_specs=(spec, spec, P()),
        check_vma=False,
    )
```

```python
import functools
import math

import jax
import jax.numpy as jnp
from jax import lax
from jax.experimental import pallas as pl
from jax.experimental.pallas import tpu as pltpu
from jax.sharding import PartitionSpec as P

HEADS = 16
HALF = 8
HD = 64
LEVELS = 3
N_LON = 16
N_LAT = 8
TOK = 192
WIDTH = 1024
BAND = 512
SCALE = 0.125
LOG2E = math.log2(math.e)
NEG = -1e30
BF = jnp.bfloat16
F32 = jnp.float32
VMEM = 32 * 1024 * 1024


def call(kernel, outs, flops, nbytes, ins, scratch=()):
    return pl.pallas_call(
        kernel,
        grid=(1,),
        in_specs=[spec for spec, _ in ins],
        out_specs=tuple(spec for spec, _ in outs),
        out_shape=tuple(shape for _, shape in outs),
        scratch_shapes=list(scratch),
        compiler_params=pltpu.CompilerParams(vmem_limit_bytes=VMEM),
        cost_estimate=pl.CostEstimate(flops=50 * flops, bytes_accessed=nbytes, transcendentals=0),
    )(*[x for _, x in ins])


def in_smem(x):
    return (pl.BlockSpec(memory_space=pltpu.SMEM), x)


def in_vmem(x):
    return (pl.BlockSpec(memory_space=pltpu.VMEM), x)


def in_hbm(x):
    return (pl.BlockSpec(memory_space=pltpu.HBM), hbm(x))


def out_vmem(shape, dtype):
    return (pl.BlockSpec(memory_space=pltpu.VMEM), pltpu.VMEM(shape, dtype))


def out_hbm(shape, dtype):
    return (pl.BlockSpec(memory_space=pltpu.HBM), pltpu.HBM(shape, dtype))


def out_block(shape, dtype):
    zeros = (0,) * len(shape)
    return (pl.BlockSpec(shape, lambda g: zeros), pltpu.HBM(shape, dtype))


def begin(pairs, sems):
    copies = [pltpu.make_async_copy(a, b, sems.at[n]) for n, (a, b) in enumerate(pairs)]
    for copy in copies:
        copy.start()
    return copies


def hbm(x):
    return pltpu.with_memory_space_constraint(x, pltpu.HBM)


def dot(a, b):
    return jnp.dot(a, b, preferred_element_type=F32)


def dot_nt(a, b):
    return lax.dot_general(a, b, (((1,), (1,)), ((), ())), preferred_element_type=F32)


def tr(x):
    return jnp.transpose(x)


def band_proj_kernel(
    tok_hbm, wq_hbm, wk_hbm, wv_hbm, out_ref, tok_ref, wq_ref, wk_ref, wv_ref, sems
):
    lanes = pl.ds(0, BAND)
    copies = begin(
        [
            (tok_hbm, tok_ref),
            (wq_hbm.at[:, lanes], wq_ref),
            (wk_hbm.at[:, lanes], wk_ref),
            (wv_hbm.at[:, lanes], wv_ref),
        ],
        sems,
    )
    copies[0].wait()
    tok = tok_ref[...]
    copies[1].wait()
    q = dot(tok, wq_ref[...]).astype(BF)
    copies[2].wait()
    k = dot(tok, wk_ref[...]).astype(BF)
    copies[3].wait()
    v = dot(tok, wv_ref[...]).astype(BF)
    for h in range(HALF):
        lanes = slice(64 * h, 64 * h + 64)
        qk = jnp.concatenate([q[:, lanes], k[:, lanes]], axis=1)
        vh = v[:, lanes]
        for l in range(LEVELS):
            for r in range(2):
                base = l * 64 + r * 32
                out_ref[2 * h + r, 48 * l : 48 * l + 32, :] = qk[base : base + 32]
                out_ref[2 * h + r, 48 * l + 32 : 48 * l + 48, :] = jnp.concatenate(
                    [vh[base : base + 16], vh[base + 16 : base + 32]], axis=1
                )


WEIGHT_HALF = pltpu.VMEM((WIDTH, BAND), BF)


def band_proj(tok, wq, wk, wv):
    return call(
        band_proj_kernel,
        [out_block((N_LON, 144, 128), BF)],
        6 * TOK * WIDTH * BAND,
        4 * 1024 * 1024,
        [in_hbm(x) for x in (tok, wq, wk, wv)],
        [pltpu.VMEM((TOK, WIDTH), BF)] + [WEIGHT_HALF] * 3 + [pltpu.SemaphoreType.DMA((4,))],
    )[0]


def unpack_qkv(x):
    qk = x[:, 0:32, :].reshape(512, 128)
    v = x[:, 32:48, :]
    v = jnp.concatenate([v[:, :, 0:64], v[:, :, 64:128]], axis=1).reshape(512, 64)
    return qk[:, 0:64], qk[:, 64:128], v


def unpack_one(x):
    return jnp.concatenate([x[:, :, 0:64], x[:, :, 64:128]], axis=1).reshape(512, 64)


def pack_one(x):
    x = x.reshape(N_LON, 32, 64)
    return jnp.concatenate([x[:, 0:16, :], x[:, 16:32, :]], axis=2)


def band_fwd_kernel(x_ref, o_ref, stat_ref):
    for l in range(LEVELS):
        q, k, v = unpack_qkv(x_ref[:, 48 * l : 48 * l + 48, :])
        s = dot_nt(k, q) * (SCALE * LOG2E)
        top = jnp.max(s, axis=0, keepdims=True)
        e = jnp.exp2(s - top)
        rtot = 1.0 / jnp.sum(e, axis=0, keepdims=True)
        w = (e * rtot).astype(BF)
        o = tr(dot(tr(v), w)).astype(BF)
        o_ref[:, 16 * l : 16 * l + 16, :] = pack_one(o)
        stat_ref[l, 0:1, :] = top
        stat_ref[l, 1:2, :] = rtot


def band_fwd(x):
    return call(
        band_fwd_kernel,
        [out_block((N_LON, 48, 128), BF), out_vmem((LEVELS, 2, 512), F32)],
        12 * 512 * 512 * 64,
        1024 * 1024,
        [in_vmem(x)],
    )


def band_bwd_kernel(x_ref, o_ref, stat_ref, do_ref, mine_ref, other_ref, out_ref):
    total = jnp.broadcast_to(mine_ref[0:1, :] + other_ref[0:1, :], (16, 128))
    high = total.astype(BF).astype(F32)
    mid = (total - high).astype(BF).astype(F32)
    low = total - high - mid
    at = lax.broadcasted_iota(jnp.int32, (16, 128), 1)
    parts = jnp.where(at == 0, high, jnp.where(at == 1, mid, jnp.where(at == 2, low, 0.0)))
    parts = parts.astype(BF)
    for j in range(N_LON):
        out_ref[j, 144:160, :] = parts
    for l in range(LEVELS):
        q, k, v = unpack_qkv(x_ref[:, 48 * l : 48 * l + 48, :])
        o = unpack_one(o_ref[:, 16 * l : 16 * l + 16, :])
        do = unpack_one(do_ref[:, 16 * l : 16 * l + 16, :])
        s = dot_nt(k, q) * (SCALE * LOG2E)
        p = jnp.exp2(s - stat_ref[l, 0:1, :]) * stat_ref[l, 1:2, :]
        w = p.astype(BF)
        dp = dot_nt(v, do)
        delta = jnp.sum(tr(do.astype(F32) * o.astype(F32)), axis=0, keepdims=True)
        ds = (p * (dp - delta) * SCALE).astype(BF)
        dv = dot(w, do).astype(BF)
        dk = dot(ds, q).astype(BF)
        dq = tr(dot(tr(k), ds)).astype(BF)
        out_ref[:, 48 * l : 48 * l + 32, :] = jnp.concatenate([dq, dk], axis=1).reshape(
            N_LON, 32, 128
        )
        out_ref[:, 48 * l + 32 : 48 * l + 48, :] = pack_one(dv)


def band_bwd(x, o, stat, do, mine, other):
    return call(
        band_bwd_kernel,
        [out_block((N_LON, 160, 128), BF)],
        30 * 512 * 512 * 64,
        2 * 1024 * 1024,
        [in_vmem(y) for y in (x, o, stat, do, mine, other)],
    )[0]


def to_halves(x):
    return jnp.concatenate(
        [x[32 * i + 16 * s : 32 * i + 16 * s + 16] for s in range(2) for i in range(6)], axis=0
    )


def from_halves(x):
    return jnp.concatenate(
        [x[96 * s + 16 * i : 96 * s + 16 * i + 16] for i in range(6) for s in range(2)], axis=0
    )


def win_proj_kernel(
    tok_hbm, wq_hbm, wk_hbm, wv_hbm, q_ref, k_ref, v_ref, tok_ref, wq_ref, wk_ref, wv_ref, sems
):
    lanes = pl.ds(BAND, BAND)
    copies = begin(
        [
            (tok_hbm, tok_ref),
            (wq_hbm.at[:, lanes], wq_ref),
            (wk_hbm.at[:, lanes], wk_ref),
            (wv_hbm.at[:, lanes], wv_ref),
        ],
        sems,
    )
    copies[0].wait()
    tok = to_halves(tok_ref[...])
    copies[1].wait()
    q_ref[...] = dot(tok, wq_ref[...]).astype(BF)
    copies[2].wait()
    k_ref[...] = dot(tok, wk_ref[...]).astype(BF)
    copies[3].wait()
    v_ref[...] = dot(tok, wv_ref[...]).astype(BF)


def win_proj(tok, wq, wk, wv):
    return call(
        win_proj_kernel,
        [out_block((TOK, BAND), BF)] * 3,
        6 * TOK * WIDTH * BAND,
        4 * 1024 * 1024,
        [in_hbm(x) for x in (tok, wq, wk, wv)],
        [pltpu.VMEM((TOK, WIDTH), BF)] + [WEIGHT_HALF] * 3 + [pltpu.SemaphoreType.DMA((4,))],
    )


def window_distance(pos):
    key = lax.broadcasted_iota(jnp.int32, (288, 96), 0)
    query = lax.broadcasted_iota(jnp.int32, (288, 96), 1)
    block = (key >= 96).astype(jnp.int32) + (key >= 192).astype(jnp.int32)
    inner = key - 96 * block
    shift = jnp.where(block == 1, -2, jnp.where(block == 2, 2, 0))
    offset = shift + ((inner >> 4) & 1) - ((query >> 4) & 1)
    allowed = (inner & 15) == (query & 15)
    allowed = allowed & ((block != 1) | (pos > 0)) & ((block != 2) | (pos < N_LAT - 1))
    return jnp.where(allowed, jnp.abs(offset), 99)


def extended(own, halo, half):
    rows = slice(96 * half, 96 * half + 96)
    nrows = slice(TOK + 96 * half, TOK + 96 * half + 96)
    return jnp.concatenate([own[rows], halo[rows], halo[nrows]], axis=0)


def win_fwd_kernel(
    pos_ref, reach_ref, prev_ref, next_ref, wk_hbm, wv_hbm, wq_hbm, q_hbm, k_hbm, v_hbm,
    o_ref, stat_ref, hq_ref, hk_ref, hv_ref,
    wk_ref, wv_ref, wq_ref, q_ref, k_ref, v_ref, sems,
):
    lanes = pl.ds(BAND, BAND)
    copies = begin(
        [
            (wk_hbm.at[:, lanes], wk_ref),
            (wv_hbm.at[:, lanes], wv_ref),
            (wq_hbm.at[:, lanes], wq_ref),
            (q_hbm, q_ref),
            (k_hbm, k_ref),
            (v_hbm, v_ref),
        ],
        sems,
    )
    dist = window_distance(pos_ref[0])
    near = jnp.concatenate([to_halves(prev_ref[...]), to_halves(next_ref[...])], axis=0)
    copies[0].wait()
    hk_ref[...] = dot(near, wk_ref[...]).astype(BF)
    copies[1].wait()
    hv_ref[...] = dot(near, wv_ref[...]).astype(BF)
    copies[2].wait()
    hq_ref[...] = dot(near, wq_ref[...]).astype(BF)
    for copy in copies[3:6]:
        copy.wait()
    for half in range(2):
        rows = slice(96 * half, 96 * half + 96)
        q = q_ref[rows]
        k = extended(k_ref[...], hk_ref[...], half)
        vt = tr(extended(v_ref[...], hv_ref[...], half))
        outs = []
        tops = []
        rtots = []
        for h in range(HALF):
            lanes = slice(64 * h, 64 * h + 64)
            s = dot_nt(k[:, lanes], q[:, lanes]) * (SCALE * LOG2E)
            s = jnp.where(dist <= reach_ref[h], s, NEG)
            top = jnp.max(s, axis=0, keepdims=True)
            e = jnp.exp2(s - top)
            rtot = 1.0 / jnp.sum(e, axis=0, keepdims=True)
            w = (e * rtot).astype(BF)
            outs.append(dot(vt[lanes], w))
            tops.append(top)
            rtots.append(rtot)
        o_ref[rows] = tr(jnp.concatenate(outs, axis=0)).astype(BF)
        stats = jnp.concatenate(tops + rtots + [jnp.zeros((112, 96), F32)], axis=0)
        stat_ref[rows] = tr(stats)

def win_fwd(pos, reach, q, k, v, prev, nxt, wq, wk, wv):
    return call(
        win_fwd_kernel,
        [
            out_vmem((TOK, BAND), BF),
            out_vmem((TOK, 128), F32),
            out_block((2 * TOK, BAND), BF),
            out_block((2 * TOK, BAND), BF),
            out_block((2 * TOK, BAND), BF),
        ],
        64 * 288 * 128 * 64 + 12 * TOK * WIDTH * BAND,
        6 * 1024 * 1024,
        [in_smem(pos), in_smem(reach)]
        + [in_vmem(prev), in_vmem(nxt)]
        + [in_hbm(x) for x in (wk, wv, wq, q, k, v)],
        [WEIGHT_HALF] * 3
        + [pltpu.VMEM((TOK, BAND), BF)] * 3
        + [pltpu.SemaphoreType.DMA((9,))],
    )


def statistics(rows):
    parts = tr(rows.astype(F32))
    return parts[0:32] + parts[32:64] + parts[64:96]


def neighbour_distance(pos):
    key = lax.broadcasted_iota(jnp.int32, (96, 192), 0)
    lane = lax.broadcasted_iota(jnp.int32, (96, 192), 1)
    after = lane >= 96
    query = lane - jnp.where(after, 96, 0)
    offset = ((key >> 4) & 1) - ((query >> 4) & 1) + jnp.where(after, -2, 2)
    allowed = (key & 15) == (query & 15)
    allowed = allowed & (after | (pos > 0)) & (~after | (pos < N_LAT - 1))
    return jnp.where(allowed, jnp.abs(offset), 99)


def win_grad_kernel(
    pos_ref, reach_ref, prev_ref, next_ref, q_hbm, k_hbm, v_hbm, hk_hbm, hv_hbm, pay_hbm, hq_hbm,
    dm_hbm, wq_hbm, wk_hbm, wv_hbm, out_ref,
    q_ref, k_ref, v_ref, hk_ref, hv_ref, pay_ref, hq_ref, dm_ref, wq_ref, wk_ref, wv_ref,
    dq_s, dk_s, dv_s, sems,
):
    window = pl.ds(BAND, BAND)
    copies = begin(
        [
            (q_hbm, q_ref),
            (k_hbm, k_ref),
            (v_hbm, v_ref),
            (hk_hbm, hk_ref),
            (hv_hbm, hv_ref),
            (pay_hbm, pay_ref),
            (hq_hbm, hq_ref),
            (wq_hbm.at[:, window], wq_ref),
            (wk_hbm.at[:, window], wk_ref),
            (wv_hbm.at[:, window], wv_ref),
            (dm_hbm, dm_ref),
        ],
        sems,
    )
    dist = window_distance(pos_ref[0])
    near_dist = neighbour_distance(pos_ref[0])
    for copy in copies[:7]:
        copy.wait()
    for half in range(2):
        rows = slice(96 * half, 96 * half + 96)
        nrows = slice(TOK + 96 * half, TOK + 96 * half + 96)
        q = q_ref[rows]
        k = extended(k_ref[...], hk_ref[...], half)
        v = extended(v_ref[...], hv_ref[...], half)
        kt = tr(k)
        do = pay_ref[rows, 0:BAND]
        stat = statistics(pay_ref[rows, BAND:])
        near_q = jnp.concatenate([hq_ref[rows], hq_ref[nrows]], axis=0)
        near_pay = jnp.concatenate([prev_ref[rows], next_ref[rows]], axis=0)
        near_do = near_pay[:, 0:BAND]
        near_stat = statistics(near_pay[:, BAND:])
        dqs = []
        for pair in range(HALF // 2):
            dks = []
            dvs = []
            for h in (2 * pair, 2 * pair + 1):
                lanes = slice(64 * h, 64 * h + 64)
                qh, kh, vh, doh = q[:, lanes], k[:, lanes], v[:, lanes], do[:, lanes]
                s = dot_nt(kh, qh) * (SCALE * LOG2E)
                e = jnp.exp2(s - stat[h : h + 1])
                p = jnp.where(dist <= reach_ref[h], e * stat[8 + h : 9 + h], 0.0)
                dp = dot_nt(vh, doh)
                ds = (p * (dp - stat[16 + h : 17 + h]) * SCALE).astype(BF)
                dqs.append(dot(kt[lanes], ds))
                qn, don = near_q[:, lanes], near_do[:, lanes]
                s = dot_nt(kh[0:96], qn) * (SCALE * LOG2E)
                e = jnp.exp2(s - near_stat[h : h + 1])
                pn = jnp.where(near_dist <= reach_ref[h], e * near_stat[8 + h : 9 + h], 0.0)
                dp = dot_nt(vh[0:96], don)
                dsn = (pn * (dp - near_stat[16 + h : 17 + h]) * SCALE).astype(BF)
                dvs.append(dot(p[0:96].astype(BF), doh) + dot(pn.astype(BF), don))
                dks.append(dot(ds[0:96], qh) + dot(dsn, qn))
            out = slice(128 * pair, 128 * pair + 128)
            dk_s[rows, out] = jnp.concatenate(dks, axis=1).astype(BF)
            dv_s[rows, out] = jnp.concatenate(dvs, axis=1).astype(BF)
        dq_s[rows] = tr(jnp.concatenate(dqs, axis=0)).astype(BF)
    for copy in copies[7:]:
        copy.wait()
    g = dot_nt(dq_s[...], wq_ref[...])
    g = g + dot_nt(dk_s[...], wk_ref[...]) + dot_nt(dv_s[...], wv_ref[...])
    out_ref[...] = dm_ref[...].astype(F32) + from_halves(g)


def win_grad(pos, reach, q, k, v, hk, hv, pay, hq, prev, nxt, dm, wq, wk, wv):
    return call(
        win_grad_kernel,
        [out_block((TOK, WIDTH), F32)],
        6 * TOK * WIDTH * BAND + 200 * 288 * 128 * 64,
        8 * 1024 * 1024,
        [in_smem(pos), in_smem(reach)]
        + [in_vmem(prev), in_vmem(nxt)]
        + [in_hbm(x) for x in (q, k, v, hk, hv, pay, hq, dm, wq, wk, wv)],
        [pltpu.VMEM((TOK, BAND), BF)] * 3
        + [
            pltpu.VMEM((2 * TOK, BAND), BF),
            pltpu.VMEM((2 * TOK, BAND), BF),
            pltpu.VMEM((TOK, BAND + 128), BF),
            pltpu.VMEM((2 * TOK, BAND), BF),
            pltpu.VMEM((TOK, WIDTH), BF),
        ]
        + [WEIGHT_HALF] * 3
        + [pltpu.VMEM((TOK, BAND), BF)] * 3
        + [pltpu.SemaphoreType.DMA((11,))],
    )[0]


def mid_kernel(
    table_ref, tok_hbm, tgt_hbm, wo_hbm, o_ref, win_ref, stat_ref,
    mixed_hbm, dm_hbm, send_ref, pay_ref, sum_ref,
    tok_ref, tgt_ref, wo_ref, mixed_ref, dm_ref, att_s, sems,
):
    copies = begin([(wo_hbm, wo_ref), (tok_hbm, tok_ref), (tgt_hbm, tgt_ref)], sems)
    for pair in range(HALF // 2):
        lanes = slice(128 * pair, 128 * pair + 128)
        for l in range(LEVELS):
            for r in range(2):
                base = 64 * l + 32 * r
                a = o_ref[4 * pair + r, 16 * l : 16 * l + 16, :]
                b = o_ref[4 * pair + 2 + r, 16 * l : 16 * l + 16, :]
                att_s[base : base + 16, lanes] = jnp.concatenate([a[:, 0:64], b[:, 0:64]], axis=1)
                att_s[base + 16 : base + 32, lanes] = jnp.concatenate(
                    [a[:, 64:128], b[:, 64:128]], axis=1
                )
    att_s[:, BAND:] = from_halves(win_ref[...])
    att = att_s[...]
    for copy in copies:
        copy.wait()
    d_att = jnp.zeros((TOK, WIDTH), F32)
    total = jnp.zeros((8, 256), F32)
    for g in range(4):
        lanes = slice(256 * g, 256 * g + 256)
        mixed = (tok_ref[:, lanes].astype(F32) + dot(att, wo_ref[:, lanes])).astype(BF)
        mixed_ref[:, lanes] = mixed
        diff = mixed.astype(F32) - tgt_ref[:, lanes].astype(F32)
        weighted = (table_ref[g].astype(F32) * 0.25) * diff
        total = total + jnp.sum((weighted * diff).reshape(TOK // 8, 8, 256), axis=0)
        dm = weighted.astype(BF)
        dm_ref[:, lanes] = dm
        d_att = d_att + dot_nt(dm, wo_ref[:, lanes])
    copies = begin([(mixed_ref, mixed_hbm), (dm_ref, dm_hbm)], sems)
    d_att = d_att.astype(BF)
    dwin = to_halves(d_att[:, BAND:])
    pay_ref[:, 0:BAND] = dwin
    terms = dwin.astype(F32) * win_ref[...].astype(F32)
    first = terms.astype(BF)
    second = (terms - first.astype(F32)).astype(BF)
    feature = lax.broadcasted_iota(jnp.int32, (BAND, 128), 0)
    lane = lax.broadcasted_iota(jnp.int32, (BAND, 128), 1)
    gather = ((feature >> 6) + 16 == lane).astype(F32).astype(BF)
    stat = stat_ref[...] + dot(first, gather) + dot(second, gather)
    high = stat.astype(BF).astype(F32)
    middle = (stat - high).astype(BF).astype(F32)
    low = stat - high - middle
    packed = high + pltpu.roll(middle, 32, 1) + pltpu.roll(low, 64, 1)
    pay_ref[:, BAND:] = packed.astype(BF)
    for h in range(HALF):
        dh = d_att[:, 64 * h : 64 * h + 64]
        for l in range(LEVELS):
            for r in range(2):
                base = 64 * l + 32 * r
                send_ref[2 * h + r, 16 * l : 16 * l + 16, :] = jnp.concatenate(
                    [dh[base : base + 16], dh[base + 16 : base + 32]], axis=1
                )
    sum_ref[...] = jnp.broadcast_to(jnp.sum(total), (8, 128))
    for copy in copies:
        copy.wait()


def mid(table, tok, tgt, o, win, stat, wo):
    return call(
        mid_kernel,
        [
            out_hbm((TOK, WIDTH), BF),
            out_hbm((TOK, WIDTH), BF),
            out_block((N_LON, 48, 128), BF),
            out_block((TOK, BAND + 128), BF),
            out_block((8, 128), F32),
        ],
        4 * TOK * WIDTH * WIDTH,
        4 * 1024 * 1024,
        [in_smem(table)]
        + [in_hbm(x) for x in (tok, tgt, wo)]
        + [in_vmem(x) for x in (o, win, stat)],
        [pltpu.VMEM((TOK, WIDTH), BF)] * 2
        + [pltpu.VMEM((WIDTH, WIDTH), BF)]
        + [pltpu.VMEM((TOK, WIDTH), BF)] * 3
        + [pltpu.SemaphoreType.DMA((3,))],
    )


def band_grad_kernel(
    x_ref, base_hbm, wq_hbm, wk_hbm, wv_hbm, out_hbm, loss_ref,
    base_ref, wq_ref, wk_ref, wv_ref, dq_s, dk_s, dv_s, out_s, sems,
):
    band = pl.ds(0, BAND)
    loads = begin(
        [
            (wq_hbm.at[:, band], wq_ref),
            (wk_hbm.at[:, band], wk_ref),
            (wv_hbm.at[:, band], wv_ref),
            (base_hbm, base_ref),
        ],
        sems,
    )
    for pair in range(HALF // 2):
        lanes = slice(128 * pair, 128 * pair + 128)
        for l in range(LEVELS):
            for r in range(2):
                base = 64 * l + 32 * r
                a = x_ref[4 * pair + r, 48 * l : 48 * l + 48, :]
                b = x_ref[4 * pair + 2 + r, 48 * l : 48 * l + 48, :]
                first = jnp.concatenate([a[:, 0:64], b[:, 0:64]], axis=1)
                second = jnp.concatenate([a[:, 64:128], b[:, 64:128]], axis=1)
                dq_s[base : base + 32, lanes] = first[0:32]
                dk_s[base : base + 32, lanes] = second[0:32]
                dv_s[base : base + 16, lanes] = first[32:48]
                dv_s[base + 16 : base + 32, lanes] = second[32:48]
    dq = dq_s[...]
    dk = dk_s[...]
    dv = dv_s[...]
    for load in loads:
        load.wait()
    copies = []
    for n in range(4):
        rows = slice(256 * n, 256 * n + 256)
        g = dot_nt(dq, wq_ref[rows, :]) + dot_nt(dk, wk_ref[rows, :])
        out_s[:, rows] = base_ref[:, rows] + g + dot_nt(dv, wv_ref[rows, :])
        lanes = pl.ds(256 * n, 256)
        copy = pltpu.make_async_copy(out_s.at[:, lanes], out_hbm.at[:, lanes], sems.at[n])
        copy.start()
        copies.append(copy)
    loss_ref[0, 0] = jnp.sum(x_ref[:, 144, :].astype(F32)) * (1.0 / 25165824)
    for copy in copies:
        copy.wait()


def band_grad(x, base, wq, wk, wv):
    return call(
        band_grad_kernel,
        [
            out_hbm((TOK, WIDTH), F32),
            (pl.BlockSpec(memory_space=pltpu.SMEM), jax.ShapeDtypeStruct((1, 1), F32)),
        ],
        6 * TOK * WIDTH * BAND,
        5 * 1024 * 1024,
        [in_vmem(x)] + [in_hbm(y) for y in (base, wq, wk, wv)],
        [pltpu.VMEM((TOK, WIDTH), F32)]
        + [WEIGHT_HALF] * 3
        + [pltpu.VMEM((TOK, BAND), BF)] * 3
        + [pltpu.VMEM((TOK, WIDTH), F32), pltpu.SemaphoreType.DMA((4,))],
    )


def swap(x):
    return lax.all_to_all(x, "lon", 0, 0, tiled=True)


UP = [(i, (i + 1) % N_LAT) for i in range(N_LAT)]
DOWN = [((i + 1) % N_LAT, i) for i in range(N_LAT)]


def per_device(tokens, targets, w_query, w_key, w_value, w_out, window_reach, loss_table):
    levels, rows, cols, width = tokens.shape
    count = levels * rows * cols
    tok = tokens.reshape(count, width)
    tgt = targets.reshape(count, width)
    pos = lax.axis_index("lat").astype(jnp.int32).reshape(1)
    with jax.named_scope("band_projection"):
        sent = band_proj(tok, w_query, w_key, w_value)
    with jax.named_scope("halo_tokens"):
        prev = lax.ppermute(tok, "lat", UP)
    with jax.named_scope("band_qkv_exchange"):
        x = swap(sent)
    with jax.named_scope("window_projection"):
        q, k, v = win_proj(tok, w_query, w_key, w_value)
        x, q, k, v, tok_later = lax.optimization_barrier((x, q, k, v, tok))
        nxt = lax.ppermute(tok_later, "lat", DOWN)
    with jax.named_scope("band_forward"):
        o, stat = band_fwd(x)
        o_back = swap(o)
    with jax.named_scope("window_forward"):
        win, wstat, hq, hk, hv = win_fwd(
            pos, window_reach, q, k, v, prev, nxt, w_query, w_key, w_value
        )
    with jax.named_scope("middle"):
        mixed, dm, dsend, pay, part = mid(loss_table, tok, tgt, o_back, win, wstat, w_out)
        losses = [part] + [
            lax.ppermute(part, "lat", [(i, i ^ step) for i in range(N_LAT)]) for step in (1, 2, 3)
        ]
        do = swap(dsend)
        pay_prev = lax.ppermute(pay, "lat", UP)
        pay_next = lax.ppermute(pay, "lat", DOWN)
    with jax.named_scope("band_backward"):
        four = losses[0] + losses[1] + losses[2] + losses[3]
        far = lax.ppermute(four, "lat", [(i, i ^ 4) for i in range(N_LAT)])
        dsent = band_bwd(x, o, stat, do, four, far)
        dx = swap(dsent)
    with jax.named_scope("window_gradient"):
        base = win_grad(
            pos, window_reach, q, k, v, hk, hv, pay, hq, pay_prev, pay_next, dm,
            w_query, w_key, w_value,
        )
    with jax.named_scope("token_gradient"):
        grad, loss = band_grad(dx, base, w_query, w_key, w_value)
    full = (levels, rows, cols, width)
    return (mixed.reshape(full), grad.reshape(full), loss.reshape(()))


def solution(mesh):
    spec = P(None, "lat", "lon", None)
    return jax.shard_map(
        per_device,
        mesh=mesh,
        in_specs=(spec, spec, P(), P(), P(), P(), P(), P()),
        out_specs=(spec, spec, P()),
        check_vma=False,
    )
```

```python
import functools
import math

import jax
import jax.numpy as jnp
from jax import lax
from jax.experimental import pallas as pl
from jax.experimental.pallas import tpu as pltpu
from jax.sharding import PartitionSpec as P

HEADS = 16
HALF = 8
HD = 64
LEVELS = 3
N_LON = 16
N_LAT = 8
TOK = 192
WIDTH = 1024
BAND = 512
SCALE = 0.125
LOG2E = math.log2(math.e)
NEG = -1e30
BF = jnp.bfloat16
F32 = jnp.float32
VMEM = 32 * 1024 * 1024


def call(kernel, outs, flops, nbytes, ins, scratch=()):
    return pl.pallas_call(
        kernel,
        grid=(1,),
        in_specs=[spec for spec, _ in ins],
        out_specs=tuple(spec for spec, _ in outs),
        out_shape=tuple(shape for _, shape in outs),
        scratch_shapes=list(scratch),
        compiler_params=pltpu.CompilerParams(vmem_limit_bytes=VMEM),
        cost_estimate=pl.CostEstimate(flops=50 * flops, bytes_accessed=nbytes, transcendentals=0),
    )(*[x for _, x in ins])


def in_smem(x):
    return (pl.BlockSpec(memory_space=pltpu.SMEM), x)


def in_vmem(x):
    return (pl.BlockSpec(memory_space=pltpu.VMEM), x)


def in_hbm(x):
    return (pl.BlockSpec(memory_space=pltpu.HBM), hbm(x))


def out_vmem(shape, dtype):
    return (pl.BlockSpec(memory_space=pltpu.VMEM), pltpu.VMEM(shape, dtype))


def out_hbm(shape, dtype):
    return (pl.BlockSpec(memory_space=pltpu.HBM), pltpu.HBM(shape, dtype))


def out_block(shape, dtype):
    zeros = (0,) * len(shape)
    return (pl.BlockSpec(shape, lambda g: zeros), pltpu.HBM(shape, dtype))


def begin(pairs, sems):
    copies = [pltpu.make_async_copy(a, b, sems.at[n]) for n, (a, b) in enumerate(pairs)]
    for copy in copies:
        copy.start()
    return copies


def hbm(x):
    return pltpu.with_memory_space_constraint(x, pltpu.HBM)


def dot(a, b):
    return jnp.dot(a, b, preferred_element_type=F32)


def dot_nt(a, b):
    return lax.dot_general(a, b, (((1,), (1,)), ((), ())), preferred_element_type=F32)


def tr(x):
    return jnp.transpose(x)


def band_proj_kernel(
    tok_hbm, wq_hbm, wk_hbm, wv_hbm, out_ref, tok_ref, wq_ref, wk_ref, wv_ref, sems
):
    lanes = pl.ds(0, BAND)
    copies = begin(
        [
            (tok_hbm, tok_ref),
            (wq_hbm.at[:, lanes], wq_ref),
            (wk_hbm.at[:, lanes], wk_ref),
            (wv_hbm.at[:, lanes], wv_ref),
        ],
        sems,
    )
    copies[0].wait()
    tok = tok_ref[...]
    copies[1].wait()
    q = dot(tok, wq_ref[...]).astype(BF)
    copies[2].wait()
    k = dot(tok, wk_ref[...]).astype(BF)
    copies[3].wait()
    v = dot(tok, wv_ref[...]).astype(BF)
    for h in range(HALF):
        lanes = slice(64 * h, 64 * h + 64)
        qk = jnp.concatenate([q[:, lanes], k[:, lanes]], axis=1)
        vh = v[:, lanes]
        for l in range(LEVELS):
            for r in range(2):
                base = l * 64 + r * 32
                out_ref[2 * h + r, 48 * l : 48 * l + 32, :] = qk[base : base + 32]
                out_ref[2 * h + r, 48 * l + 32 : 48 * l + 48, :] = jnp.concatenate(
                    [vh[base : base + 16], vh[base + 16 : base + 32]], axis=1
                )


WEIGHT_HALF = pltpu.VMEM((WIDTH, BAND), BF)


def band_proj(tok, wq, wk, wv):
    return call(
        band_proj_kernel,
        [out_block((N_LON, 144, 128), BF)],
        6 * TOK * WIDTH * BAND,
        4 * 1024 * 1024,
        [in_hbm(x) for x in (tok, wq, wk, wv)],
        [pltpu.VMEM((TOK, WIDTH), BF)] + [WEIGHT_HALF] * 3 + [pltpu.SemaphoreType.DMA((4,))],
    )[0]


def unpack_qkv(x):
    qk = x[:, 0:32, :].reshape(512, 128)
    v = x[:, 32:48, :]
    v = jnp.concatenate([v[:, :, 0:64], v[:, :, 64:128]], axis=1).reshape(512, 64)
    return qk[:, 0:64], qk[:, 64:128], v


def unpack_one(x):
    return jnp.concatenate([x[:, :, 0:64], x[:, :, 64:128]], axis=1).reshape(512, 64)


def pack_one(x):
    x = x.reshape(N_LON, 32, 64)
    return jnp.concatenate([x[:, 0:16, :], x[:, 16:32, :]], axis=2)


def band_fwd_kernel(x_ref, o_ref, stat_ref):
    for l in range(LEVELS):
        q, k, v = unpack_qkv(x_ref[:, 48 * l : 48 * l + 48, :])
        s = dot_nt(k, q) * (SCALE * LOG2E)
        top = jnp.max(s, axis=0, keepdims=True)
        e = jnp.exp2(s - top)
        rtot = 1.0 / jnp.sum(e, axis=0, keepdims=True)
        w = (e * rtot).astype(BF)
        o = tr(dot(tr(v), w)).astype(BF)
        o_ref[:, 16 * l : 16 * l + 16, :] = pack_one(o)
        stat_ref[l, 0:1, :] = top
        stat_ref[l, 1:2, :] = rtot


def band_fwd(x):
    return call(
        band_fwd_kernel,
        [out_block((N_LON, 48, 128), BF), out_vmem((LEVELS, 2, 512), F32)],
        12 * 512 * 512 * 64,
        1024 * 1024,
        [in_vmem(x)],
    )


def band_bwd_kernel(x_ref, o_ref, stat_ref, do_ref, mine_ref, other_ref, out_ref):
    total = jnp.broadcast_to(mine_ref[0:1, :] + other_ref[0:1, :], (16, 128))
    high = total.astype(BF).astype(F32)
    mid = (total - high).astype(BF).astype(F32)
    low = total - high - mid
    at = lax.broadcasted_iota(jnp.int32, (16, 128), 1)
    parts = jnp.where(at == 0, high, jnp.where(at == 1, mid, jnp.where(at == 2, low, 0.0)))
    parts = parts.astype(BF)
    for j in range(N_LON):
        out_ref[j, 144:160, :] = parts
    for l in range(LEVELS):
        q, k, v = unpack_qkv(x_ref[:, 48 * l : 48 * l + 48, :])
        o = unpack_one(o_ref[:, 16 * l : 16 * l + 16, :])
        do = unpack_one(do_ref[:, 16 * l : 16 * l + 16, :])
        s = dot_nt(k, q) * (SCALE * LOG2E)
        p = jnp.exp2(s - stat_ref[l, 0:1, :]) * stat_ref[l, 1:2, :]
        w = p.astype(BF)
        dp = dot_nt(v, do)
        delta = jnp.sum(tr(do.astype(F32) * o.astype(F32)), axis=0, keepdims=True)
        ds = (p * (dp - delta) * SCALE).astype(BF)
        dv = dot(w, do).astype(BF)
        dk = dot(ds, q).astype(BF)
        dq = tr(dot(tr(k), ds)).astype(BF)
        out_ref[:, 48 * l : 48 * l + 32, :] = jnp.concatenate([dq, dk], axis=1).reshape(
            N_LON, 32, 128
        )
        out_ref[:, 48 * l + 32 : 48 * l + 48, :] = pack_one(dv)


def band_bwd(x, o, stat, do, mine, other):
    return call(
        band_bwd_kernel,
        [out_block((N_LON, 160, 128), BF)],
        30 * 512 * 512 * 64,
        2 * 1024 * 1024,
        [in_vmem(y) for y in (x, o, stat, do, mine, other)],
    )[0]


def to_halves(x):
    return jnp.concatenate(
        [x[32 * i + 16 * s : 32 * i + 16 * s + 16] for s in range(2) for i in range(6)], axis=0
    )


def from_halves(x):
    return jnp.concatenate(
        [x[96 * s + 16 * i : 96 * s + 16 * i + 16] for i in range(6) for s in range(2)], axis=0
    )


def win_proj_kernel(
    prev_ref, tok_hbm, wq_hbm, wk_hbm, wv_hbm, q_ref, k_ref, v_ref,
    tok_ref, wq_ref, wk_ref, wv_ref, sems,
):
    lanes = pl.ds(BAND, BAND)
    copies = begin(
        [
            (tok_hbm, tok_ref),
            (wq_hbm.at[:, lanes], wq_ref),
            (wk_hbm.at[:, lanes], wk_ref),
            (wv_hbm.at[:, lanes], wv_ref),
        ],
        sems,
    )
    copies[0].wait()
    tok = jnp.concatenate([to_halves(tok_ref[...]), to_halves(prev_ref[...])], axis=0)
    copies[1].wait()
    q_ref[...] = dot(tok, wq_ref[...]).astype(BF)
    copies[2].wait()
    k_ref[...] = dot(tok, wk_ref[...]).astype(BF)
    copies[3].wait()
    v_ref[...] = dot(tok, wv_ref[...]).astype(BF)


def win_proj(tok, prev, wq, wk, wv):
    return call(
        win_proj_kernel,
        [out_block((2 * TOK, BAND), BF)] * 3,
        12 * TOK * WIDTH * BAND,
        4 * 1024 * 1024,
        [in_vmem(prev)] + [in_hbm(x) for x in (tok, wq, wk, wv)],
        [pltpu.VMEM((TOK, WIDTH), BF)] + [WEIGHT_HALF] * 3 + [pltpu.SemaphoreType.DMA((4,))],
    )


def window_distance(pos):
    key = lax.broadcasted_iota(jnp.int32, (288, 96), 0)
    query = lax.broadcasted_iota(jnp.int32, (288, 96), 1)
    block = (key >= 96).astype(jnp.int32) + (key >= 192).astype(jnp.int32)
    inner = key - 96 * block
    shift = jnp.where(block == 1, -2, jnp.where(block == 2, 2, 0))
    offset = shift + ((inner >> 4) & 1) - ((query >> 4) & 1)
    allowed = (inner & 15) == (query & 15)
    allowed = allowed & ((block != 1) | (pos > 0)) & ((block != 2) | (pos < N_LAT - 1))
    return jnp.where(allowed, jnp.abs(offset), 99)


def extended(two, nxt, half):
    rows = slice(96 * half, 96 * half + 96)
    prows = slice(TOK + 96 * half, TOK + 96 * half + 96)
    return jnp.concatenate([two[rows], two[prows], nxt[rows]], axis=0)


def win_fwd_kernel(
    pos_ref, reach_ref, next_ref, wk_hbm, wv_hbm, wq_hbm, q_hbm, k_hbm, v_hbm,
    o_ref, stat_ref, hq_ref, hk_ref, hv_ref,
    wk_ref, wv_ref, wq_ref, q_ref, k_ref, v_ref, sems,
):
    lanes = pl.ds(BAND, BAND)
    copies = begin(
        [
            (wk_hbm.at[:, lanes], wk_ref),
            (wv_hbm.at[:, lanes], wv_ref),
            (wq_hbm.at[:, lanes], wq_ref),
            (q_hbm, q_ref),
            (k_hbm, k_ref),
            (v_hbm, v_ref),
        ],
        sems,
    )
    dist = window_distance(pos_ref[0])
    near = to_halves(next_ref[...])
    copies[0].wait()
    hk_ref[...] = dot(near, wk_ref[...]).astype(BF)
    copies[1].wait()
    hv_ref[...] = dot(near, wv_ref[...]).astype(BF)
    copies[2].wait()
    hq_ref[...] = dot(near, wq_ref[...]).astype(BF)
    for copy in copies[3:6]:
        copy.wait()
    for half in range(2):
        rows = slice(96 * half, 96 * half + 96)
        q = q_ref[rows]
        k = extended(k_ref[...], hk_ref[...], half)
        vt = tr(extended(v_ref[...], hv_ref[...], half))
        outs = []
        tops = []
        rtots = []
        for h in range(HALF):
            lanes = slice(64 * h, 64 * h + 64)
            s = dot_nt(k[:, lanes], q[:, lanes]) * (SCALE * LOG2E)
            s = jnp.where(dist <= reach_ref[h], s, NEG)
            top = jnp.max(s, axis=0, keepdims=True)
            e = jnp.exp2(s - top)
            rtot = 1.0 / jnp.sum(e, axis=0, keepdims=True)
            w = (e * rtot).astype(BF)
            outs.append(dot(vt[lanes], w))
            tops.append(top)
            rtots.append(rtot)
        o_ref[rows] = tr(jnp.concatenate(outs, axis=0)).astype(BF)
        stats = jnp.concatenate(tops + rtots + [jnp.zeros((112, 96), F32)], axis=0)
        stat_ref[rows] = tr(stats)

def win_fwd(pos, reach, q, k, v, nxt, wq, wk, wv):
    return call(
        win_fwd_kernel,
        [
            out_block((TOK, BAND), BF),
            out_block((TOK, 128), F32),
            out_block((TOK, BAND), BF),
            out_block((TOK, BAND), BF),
            out_block((TOK, BAND), BF),
        ],
        64 * 288 * 128 * 64 + 6 * TOK * WIDTH * BAND,
        6 * 1024 * 1024,
        [in_smem(pos), in_smem(reach)]
        + [in_vmem(nxt)]
        + [in_hbm(x) for x in (wk, wv, wq, q, k, v)],
        [WEIGHT_HALF] * 3
        + [pltpu.VMEM((2 * TOK, BAND), BF)] * 3
        + [pltpu.SemaphoreType.DMA((6,))],
    )


def statistics(rows):
    parts = tr(rows.astype(F32))
    return parts[0:32] + parts[32:64] + parts[64:96]


def neighbour_distance(pos):
    key = lax.broadcasted_iota(jnp.int32, (96, 192), 0)
    lane = lax.broadcasted_iota(jnp.int32, (96, 192), 1)
    after = lane >= 96
    query = lane - jnp.where(after, 96, 0)
    offset = ((key >> 4) & 1) - ((query >> 4) & 1) + jnp.where(after, -2, 2)
    allowed = (key & 15) == (query & 15)
    allowed = allowed & (after | (pos > 0)) & (~after | (pos < N_LAT - 1))
    return jnp.where(allowed, jnp.abs(offset), 99)


def win_grad_kernel(
    pos_ref, reach_ref, prev_ref, next_ref, q_hbm, k_hbm, v_hbm, hk_hbm, hv_hbm, pay_hbm, hq_hbm,
    dm_hbm, wq_hbm, wk_hbm, wv_hbm, out_ref,
    q_ref, k_ref, v_ref, hk_ref, hv_ref, pay_ref, hq_ref, dm_ref, wq_ref, wk_ref, wv_ref,
    dq_s, dk_s, dv_s, sems,
):
    window = pl.ds(BAND, BAND)
    copies = begin(
        [
            (q_hbm, q_ref),
            (k_hbm, k_ref),
            (v_hbm, v_ref),
            (hk_hbm, hk_ref),
            (hv_hbm, hv_ref),
            (pay_hbm, pay_ref),
            (hq_hbm, hq_ref),
            (wq_hbm.at[:, window], wq_ref),
            (wk_hbm.at[:, window], wk_ref),
            (wv_hbm.at[:, window], wv_ref),
            (dm_hbm, dm_ref),
        ],
        sems,
    )
    dist = window_distance(pos_ref[0])
    near_dist = neighbour_distance(pos_ref[0])
    for copy in copies[:7]:
        copy.wait()
    for half in range(2):
        rows = slice(96 * half, 96 * half + 96)
        prows = slice(TOK + 96 * half, TOK + 96 * half + 96)
        q = q_ref[rows]
        k = extended(k_ref[...], hk_ref[...], half)
        v = extended(v_ref[...], hv_ref[...], half)
        kt = tr(k)
        do = pay_ref[rows, 0:BAND]
        stat = statistics(pay_ref[rows, BAND:])
        near_q = jnp.concatenate([q_ref[prows], hq_ref[rows]], axis=0)
        near_pay = jnp.concatenate([prev_ref[rows], next_ref[rows]], axis=0)
        near_do = near_pay[:, 0:BAND]
        near_stat = statistics(near_pay[:, BAND:])
        dqs = []
        for pair in range(HALF // 2):
            dks = []
            dvs = []
            for h in (2 * pair, 2 * pair + 1):
                lanes = slice(64 * h, 64 * h + 64)
                qh, kh, vh, doh = q[:, lanes], k[:, lanes], v[:, lanes], do[:, lanes]
                s = dot_nt(kh, qh) * (SCALE * LOG2E)
                e = jnp.exp2(s - stat[h : h + 1])
                p = jnp.where(dist <= reach_ref[h], e * stat[8 + h : 9 + h], 0.0)
                dp = dot_nt(vh, doh)
                ds = (p * (dp - stat[16 + h : 17 + h]) * SCALE).astype(BF)
                dqs.append(dot(kt[lanes], ds))
                qn, don = near_q[:, lanes], near_do[:, lanes]
                s = dot_nt(kh[0:96], qn) * (SCALE * LOG2E)
                e = jnp.exp2(s - near_stat[h : h + 1])
                pn = jnp.where(near_dist <= reach_ref[h], e * near_stat[8 + h : 9 + h], 0.0)
                dp = dot_nt(vh[0:96], don)
                dsn = (pn * (dp - near_stat[16 + h : 17 + h]) * SCALE).astype(BF)
                dvs.append(dot(p[0:96].astype(BF), doh) + dot(pn.astype(BF), don))
                dks.append(dot(ds[0:96], qh) + dot(dsn, qn))
            out = slice(128 * pair, 128 * pair + 128)
            dk_s[rows, out] = jnp.concatenate(dks, axis=1).astype(BF)
            dv_s[rows, out] = jnp.concatenate(dvs, axis=1).astype(BF)
        dq_s[rows] = tr(jnp.concatenate(dqs, axis=0)).astype(BF)
    for copy in copies[7:]:
        copy.wait()
    g = dot_nt(dq_s[...], wq_ref[...])
    g = g + dot_nt(dk_s[...], wk_ref[...]) + dot_nt(dv_s[...], wv_ref[...])
    out_ref[...] = dm_ref[...].astype(F32) + from_halves(g)


def win_grad(pos, reach, q, k, v, hk, hv, pay, hq, prev, nxt, dm, wq, wk, wv):
    return call(
        win_grad_kernel,
        [out_block((TOK, WIDTH), F32)],
        6 * TOK * WIDTH * BAND + 200 * 288 * 128 * 64,
        8 * 1024 * 1024,
        [in_smem(pos), in_smem(reach)]
        + [in_vmem(prev), in_vmem(nxt)]
        + [in_hbm(x) for x in (q, k, v, hk, hv, pay, hq, dm, wq, wk, wv)],
        [pltpu.VMEM((2 * TOK, BAND), BF)] * 3
        + [
            pltpu.VMEM((TOK, BAND), BF),
            pltpu.VMEM((TOK, BAND), BF),
            pltpu.VMEM((TOK, BAND + 128), BF),
            pltpu.VMEM((TOK, BAND), BF),
            pltpu.VMEM((TOK, WIDTH), BF),
        ]
        + [WEIGHT_HALF] * 3
        + [pltpu.VMEM((TOK, BAND), BF)] * 3
        + [pltpu.SemaphoreType.DMA((11,))],
    )[0]


def mid_kernel(
    table_ref, tok_hbm, tgt_hbm, win_hbm, stat_hbm, wo_ref, o_ref,
    mixed_hbm, dm_hbm, send_ref, pay_ref, sum_ref,
    tok_ref, tgt_ref, win_ref, stat_ref, mixed_ref, dm_ref, att_s, sems,
):
    copies = begin(
        [(win_hbm, win_ref), (tok_hbm, tok_ref), (tgt_hbm, tgt_ref), (stat_hbm, stat_ref)], sems
    )
    for pair in range(HALF // 2):
        lanes = slice(128 * pair, 128 * pair + 128)
        for l in range(LEVELS):
            for r in range(2):
                base = 64 * l + 32 * r
                a = o_ref[4 * pair + r, 16 * l : 16 * l + 16, :]
                b = o_ref[4 * pair + 2 + r, 16 * l : 16 * l + 16, :]
                att_s[base : base + 16, lanes] = jnp.concatenate([a[:, 0:64], b[:, 0:64]], axis=1)
                att_s[base + 16 : base + 32, lanes] = jnp.concatenate(
                    [a[:, 64:128], b[:, 64:128]], axis=1
                )
    copies[0].wait()
    att_s[:, BAND:] = from_halves(win_ref[...])
    att = att_s[...]
    for copy in copies[1:]:
        copy.wait()
    d_att = jnp.zeros((TOK, WIDTH), F32)
    total = jnp.zeros((8, 256), F32)
    for g in range(4):
        lanes = slice(256 * g, 256 * g + 256)
        mixed = (tok_ref[:, lanes].astype(F32) + dot(att, wo_ref[:, lanes])).astype(BF)
        mixed_ref[:, lanes] = mixed
        diff = mixed.astype(F32) - tgt_ref[:, lanes].astype(F32)
        weighted = (table_ref[g].astype(F32) * 0.25) * diff
        total = total + jnp.sum((weighted * diff).reshape(TOK // 8, 8, 256), axis=0)
        dm = weighted.astype(BF)
        dm_ref[:, lanes] = dm
        d_att = d_att + dot_nt(dm, wo_ref[:, lanes])
    copies = begin([(mixed_ref, mixed_hbm), (dm_ref, dm_hbm)], sems)
    d_att = d_att.astype(BF)
    dwin = to_halves(d_att[:, BAND:])
    pay_ref[:, 0:BAND] = dwin
    terms = dwin.astype(F32) * win_ref[...].astype(F32)
    first = terms.astype(BF)
    second = (terms - first.astype(F32)).astype(BF)
    feature = lax.broadcasted_iota(jnp.int32, (BAND, 128), 0)
    lane = lax.broadcasted_iota(jnp.int32, (BAND, 128), 1)
    gather = ((feature >> 6) + 16 == lane).astype(F32).astype(BF)
    stat = stat_ref[...] + dot(first, gather) + dot(second, gather)
    high = stat.astype(BF).astype(F32)
    middle = (stat - high).astype(BF).astype(F32)
    low = stat - high - middle
    packed = high + pltpu.roll(middle, 32, 1) + pltpu.roll(low, 64, 1)
    pay_ref[:, BAND:] = packed.astype(BF)
    for h in range(HALF):
        dh = d_att[:, 64 * h : 64 * h + 64]
        for l in range(LEVELS):
            for r in range(2):
                base = 64 * l + 32 * r
                send_ref[2 * h + r, 16 * l : 16 * l + 16, :] = jnp.concatenate(
                    [dh[base : base + 16], dh[base + 16 : base + 32]], axis=1
                )
    sum_ref[...] = jnp.broadcast_to(jnp.sum(total), (8, 128))
    for copy in copies:
        copy.wait()


def mid(table, tok, tgt, o, win, stat, wo):
    return call(
        mid_kernel,
        [
            out_hbm((TOK, WIDTH), BF),
            out_hbm((TOK, WIDTH), BF),
            out_block((N_LON, 48, 128), BF),
            out_block((TOK, BAND + 128), BF),
            out_block((8, 128), F32),
        ],
        4 * TOK * WIDTH * WIDTH,
        4 * 1024 * 1024,
        [in_smem(table)]
        + [in_hbm(x) for x in (tok, tgt, win, stat)]
        + [in_vmem(x) for x in (wo, o)],
        [pltpu.VMEM((TOK, WIDTH), BF)] * 2
        + [pltpu.VMEM((TOK, BAND), BF), pltpu.VMEM((TOK, 128), F32)]
        + [pltpu.VMEM((TOK, WIDTH), BF)] * 3
        + [pltpu.SemaphoreType.DMA((4,))],
    )


def band_grad_kernel(
    x_ref, base_hbm, wq_hbm, wk_hbm, wv_hbm, out_hbm, loss_ref,
    base_ref, wq_ref, wk_ref, wv_ref, dq_s, dk_s, dv_s, out_s, sems,
):
    band = pl.ds(0, BAND)
    loads = begin(
        [
            (wq_hbm.at[:, band], wq_ref),
            (wk_hbm.at[:, band], wk_ref),
            (wv_hbm.at[:, band], wv_ref),
            (base_hbm, base_ref),
        ],
        sems,
    )
    for pair in range(HALF // 2):
        lanes = slice(128 * pair, 128 * pair + 128)
        for l in range(LEVELS):
            for r in range(2):
                base = 64 * l + 32 * r
                a = x_ref[4 * pair + r, 48 * l : 48 * l + 48, :]
                b = x_ref[4 * pair + 2 + r, 48 * l : 48 * l + 48, :]
                first = jnp.concatenate([a[:, 0:64], b[:, 0:64]], axis=1)
                second = jnp.concatenate([a[:, 64:128], b[:, 64:128]], axis=1)
                dq_s[base : base + 32, lanes] = first[0:32]
                dk_s[base : base + 32, lanes] = second[0:32]
                dv_s[base : base + 16, lanes] = first[32:48]
                dv_s[base + 16 : base + 32, lanes] = second[32:48]
    dq = dq_s[...]
    dk = dk_s[...]
    dv = dv_s[...]
    loads[0].wait()
    out_s[...] = dot_nt(dq, wq_ref[...])
    loads[1].wait()
    out_s[...] += dot_nt(dk, wk_ref[...])
    loads[2].wait()
    loads[3].wait()
    copies = []
    for n in range(4):
        rows = slice(256 * n, 256 * n + 256)
        out_s[:, rows] += base_ref[:, rows] + dot_nt(dv, wv_ref[rows, :])
        lanes = pl.ds(256 * n, 256)
        copy = pltpu.make_async_copy(out_s.at[:, lanes], out_hbm.at[:, lanes], sems.at[n])
        copy.start()
        copies.append(copy)
    loss_ref[0, 0] = jnp.sum(x_ref[:, 144, :].astype(F32)) * (1.0 / 25165824)
    for copy in copies:
        copy.wait()


def band_grad(x, base, wq, wk, wv):
    return call(
        band_grad_kernel,
        [
            out_hbm((TOK, WIDTH), F32),
            (pl.BlockSpec(memory_space=pltpu.SMEM), jax.ShapeDtypeStruct((1, 1), F32)),
        ],
        6 * TOK * WIDTH * BAND,
        5 * 1024 * 1024,
        [in_vmem(x)] + [in_hbm(y) for y in (base, wq, wk, wv)],
        [pltpu.VMEM((TOK, WIDTH), F32)]
        + [WEIGHT_HALF] * 3
        + [pltpu.VMEM((TOK, BAND), BF)] * 3
        + [pltpu.VMEM((TOK, WIDTH), F32), pltpu.SemaphoreType.DMA((4,))],
    )


def swap(x):
    return lax.all_to_all(x, "lon", 0, 0, tiled=True)


UP = [(i, (i + 1) % N_LAT) for i in range(N_LAT)]
DOWN = [((i + 1) % N_LAT, i) for i in range(N_LAT)]


def per_device(tokens, targets, w_query, w_key, w_value, w_out, window_reach, loss_table):
    levels, rows, cols, width = tokens.shape
    count = levels * rows * cols
    tok = tokens.reshape(count, width)
    tgt = targets.reshape(count, width)
    pos = lax.axis_index("lat").astype(jnp.int32).reshape(1)
    with jax.named_scope("band_projection"):
        sent = band_proj(tok, w_query, w_key, w_value)
    with jax.named_scope("halo_tokens"):
        prev = lax.ppermute(tok, "lat", UP)
    with jax.named_scope("band_qkv_exchange"):
        x = swap(sent)
    with jax.named_scope("window_projection"):
        q, k, v = win_proj(tok, prev, w_query, w_key, w_value)
        x, q, k, v, tok_later = lax.optimization_barrier((x, q, k, v, tok))
        nxt = lax.ppermute(tok_later, "lat", DOWN)
    with jax.named_scope("band_forward"):
        o, stat = band_fwd(x)
        o_back = swap(o)
    with jax.named_scope("window_forward"):
        win, wstat, hq, hk, hv = win_fwd(
            pos, window_reach, q, k, v, nxt, w_query, w_key, w_value
        )
    with jax.named_scope("middle"):
        mixed, dm, dsend, pay, part = mid(loss_table, tok, tgt, o_back, win, wstat, w_out)
        do = swap(dsend)
        pay_prev = lax.ppermute(pay, "lat", UP)
        pay_next = lax.ppermute(pay, "lat", DOWN)
        losses = [part] + [
            lax.ppermute(part, "lat", [(i, i ^ step) for i in range(N_LAT)]) for step in (1, 2, 3)
        ]
    with jax.named_scope("band_backward"):
        four = losses[0] + losses[1] + losses[2] + losses[3]
        far = lax.ppermute(four, "lat", [(i, i ^ 4) for i in range(N_LAT)])
        dsent = band_bwd(x, o, stat, do, four, far)
        dx = swap(dsent)
    with jax.named_scope("window_gradient"):
        base = win_grad(
            pos, window_reach, q, k, v, hk, hv, pay, hq, pay_prev, pay_next, dm,
            w_query, w_key, w_value,
        )
    with jax.named_scope("token_gradient"):
        grad, loss = band_grad(dx, base, w_query, w_key, w_value)
    full = (levels, rows, cols, width)
    return (mixed.reshape(full), grad.reshape(full), loss.reshape(()))


def solution(mesh):
    spec = P(None, "lat", "lon", None)
    return jax.shard_map(
        per_device,
        mesh=mesh,
        in_specs=(spec, spec, P(), P(), P(), P(), P(), P()),
        out_specs=(spec, spec, P()),
        check_vma=False,
    )
```

```python
import functools
import math

import jax
import jax.numpy as jnp
from jax import lax
from jax.experimental import pallas as pl
from jax.experimental.pallas import tpu as pltpu
from jax.sharding import PartitionSpec as P

HEADS = 16
HALF = 8
HD = 64
LEVELS = 3
N_LON = 16
N_LAT = 8
TOK = 192
WIDTH = 1024
BAND = 512
SCALE = 0.125
LOG2E = math.log2(math.e)
NEG = -1e30
BF = jnp.bfloat16
F32 = jnp.float32
VMEM = 32 * 1024 * 1024


def call(kernel, outs, flops, nbytes, ins, scratch=()):
    return pl.pallas_call(
        kernel,
        grid=(1,),
        in_specs=[spec for spec, _ in ins],
        out_specs=tuple(spec for spec, _ in outs),
        out_shape=tuple(shape for _, shape in outs),
        scratch_shapes=list(scratch),
        compiler_params=pltpu.CompilerParams(vmem_limit_bytes=VMEM),
        cost_estimate=pl.CostEstimate(flops=50 * flops, bytes_accessed=nbytes, transcendentals=0),
    )(*[x for _, x in ins])


def in_smem(x):
    return (pl.BlockSpec(memory_space=pltpu.SMEM), x)


def in_vmem(x):
    return (pl.BlockSpec(memory_space=pltpu.VMEM), x)


def in_hbm(x):
    return (pl.BlockSpec(memory_space=pltpu.HBM), hbm(x))


def out_vmem(shape, dtype):
    return (pl.BlockSpec(memory_space=pltpu.VMEM), pltpu.VMEM(shape, dtype))


def out_hbm(shape, dtype):
    return (pl.BlockSpec(memory_space=pltpu.HBM), pltpu.HBM(shape, dtype))


def out_block(shape, dtype):
    zeros = (0,) * len(shape)
    return (pl.BlockSpec(shape, lambda g: zeros), pltpu.HBM(shape, dtype))


def begin(pairs, sems):
    copies = [pltpu.make_async_copy(a, b, sems.at[n]) for n, (a, b) in enumerate(pairs)]
    for copy in copies:
        copy.start()
    return copies


def hbm(x):
    return pltpu.with_memory_space_constraint(x, pltpu.HBM)


def dot(a, b):
    return jnp.dot(a, b, preferred_element_type=F32)


def dot_nt(a, b):
    return lax.dot_general(a, b, (((1,), (1,)), ((), ())), preferred_element_type=F32)


def tr(x):
    return jnp.transpose(x)


def band_proj_kernel(
    tok_hbm, wq_hbm, wk_hbm, wv_hbm, out_ref, tok_ref, wq_ref, wk_ref, wv_ref, sems
):
    lanes = pl.ds(0, BAND)
    copies = begin(
        [
            (tok_hbm, tok_ref),
            (wq_hbm.at[:, lanes], wq_ref),
            (wk_hbm.at[:, lanes], wk_ref),
            (wv_hbm.at[:, lanes], wv_ref),
        ],
        sems,
    )
    copies[0].wait()
    tok = tok_ref[...]
    copies[1].wait()
    q = dot(tok, wq_ref[...]).astype(BF)
    copies[2].wait()
    k = dot(tok, wk_ref[...]).astype(BF)
    copies[3].wait()
    v = dot(tok, wv_ref[...]).astype(BF)
    for h in range(HALF):
        lanes = slice(64 * h, 64 * h + 64)
        qk = jnp.concatenate([q[:, lanes], k[:, lanes]], axis=1)
        vh = v[:, lanes]
        for l in range(LEVELS):
            for r in range(2):
                base = l * 64 + r * 32
                out_ref[2 * h + r, 48 * l : 48 * l + 32, :] = qk[base : base + 32]
                out_ref[2 * h + r, 48 * l + 32 : 48 * l + 48, :] = jnp.concatenate(
                    [vh[base : base + 16], vh[base + 16 : base + 32]], axis=1
                )


WEIGHT_HALF = pltpu.VMEM((WIDTH, BAND), BF)


def band_proj(tok, wq, wk, wv):
    return call(
        band_proj_kernel,
        [out_block((N_LON, 144, 128), BF)],
        6 * TOK * WIDTH * BAND,
        4 * 1024 * 1024,
        [in_hbm(x) for x in (tok, wq, wk, wv)],
        [pltpu.VMEM((TOK, WIDTH), BF)] + [WEIGHT_HALF] * 3 + [pltpu.SemaphoreType.DMA((4,))],
    )[0]


def unpack_qkv(x):
    qk = x[:, 0:32, :].reshape(512, 128)
    v = x[:, 32:48, :]
    v = jnp.concatenate([v[:, :, 0:64], v[:, :, 64:128]], axis=1).reshape(512, 64)
    return qk[:, 0:64], qk[:, 64:128], v


def unpack_one(x):
    return jnp.concatenate([x[:, :, 0:64], x[:, :, 64:128]], axis=1).reshape(512, 64)


def pack_one(x):
    x = x.reshape(N_LON, 32, 64)
    return jnp.concatenate([x[:, 0:16, :], x[:, 16:32, :]], axis=2)


def band_fwd_kernel(x_ref, o_ref, stat_ref):
    for l in range(LEVELS):
        q, k, v = unpack_qkv(x_ref[:, 48 * l : 48 * l + 48, :])
        s = dot_nt(k, q) * (SCALE * LOG2E)
        top = jnp.max(s, axis=0, keepdims=True)
        e = jnp.exp2(s - top)
        rtot = 1.0 / jnp.sum(e, axis=0, keepdims=True)
        w = (e * rtot).astype(BF)
        o = tr(dot(tr(v), w)).astype(BF)
        o_ref[:, 16 * l : 16 * l + 16, :] = pack_one(o)
        stat_ref[l, 0:1, :] = top
        stat_ref[l, 1:2, :] = rtot


def band_fwd(x):
    return call(
        band_fwd_kernel,
        [out_block((N_LON, 48, 128), BF), out_vmem((LEVELS, 2, 512), F32)],
        12 * 512 * 512 * 64,
        1024 * 1024,
        [in_vmem(x)],
    )


def band_bwd_kernel(x_ref, o_ref, stat_ref, do_ref, mine_ref, other_ref, out_hbm, out_ref, sems):
    total = jnp.broadcast_to(mine_ref[0:1, :] + other_ref[0:1, :], (16, 128))
    high = total.astype(BF).astype(F32)
    mid = (total - high).astype(BF).astype(F32)
    low = total - high - mid
    at = lax.broadcasted_iota(jnp.int32, (16, 128), 1)
    parts = jnp.where(at == 0, high, jnp.where(at == 1, mid, jnp.where(at == 2, low, 0.0)))
    parts = parts.astype(BF)
    for j in range(N_LON):
        out_ref[j, 144:160, :] = parts
    rows = pl.ds(144, 16)
    stores = begin([(out_ref.at[:, rows], out_hbm.at[:, rows])], sems.at[pl.ds(3, 1)])
    for l in range(LEVELS):
        q, k, v = unpack_qkv(x_ref[:, 48 * l : 48 * l + 48, :])
        o = unpack_one(o_ref[:, 16 * l : 16 * l + 16, :])
        do = unpack_one(do_ref[:, 16 * l : 16 * l + 16, :])
        s = dot_nt(k, q) * (SCALE * LOG2E)
        p = jnp.exp2(s - stat_ref[l, 0:1, :]) * stat_ref[l, 1:2, :]
        w = p.astype(BF)
        dp = dot_nt(v, do)
        delta = jnp.sum(tr(do.astype(F32) * o.astype(F32)), axis=0, keepdims=True)
        ds = (p * (dp - delta) * SCALE).astype(BF)
        dv = dot(w, do).astype(BF)
        dk = dot(ds, q).astype(BF)
        dq = tr(dot(tr(k), ds)).astype(BF)
        out_ref[:, 48 * l : 48 * l + 32, :] = jnp.concatenate([dq, dk], axis=1).reshape(
            N_LON, 32, 128
        )
        out_ref[:, 48 * l + 32 : 48 * l + 48, :] = pack_one(dv)
        rows = pl.ds(48 * l, 48)
        stores += begin([(out_ref.at[:, rows], out_hbm.at[:, rows])], sems.at[pl.ds(l, 1)])
    for store in stores:
        store.wait()


def band_bwd(x, o, stat, do, mine, other):
    return call(
        band_bwd_kernel,
        [out_hbm((N_LON, 160, 128), BF)],
        30 * 512 * 512 * 64,
        2 * 1024 * 1024,
        [in_vmem(y) for y in (x, o, stat, do, mine, other)],
        [pltpu.VMEM((N_LON, 160, 128), BF), pltpu.SemaphoreType.DMA((4,))],
    )[0]


def to_halves(x):
    return jnp.concatenate(
        [x[32 * i + 16 * s : 32 * i + 16 * s + 16] for s in range(2) for i in range(6)], axis=0
    )


def from_halves(x):
    return jnp.concatenate(
        [x[96 * s + 16 * i : 96 * s + 16 * i + 16] for i in range(6) for s in range(2)], axis=0
    )


def win_proj_kernel(
    prev_ref, tok_hbm, wq_hbm, wk_hbm, wv_hbm, q_ref, k_ref, v_ref,
    tok_ref, wq_ref, wk_ref, wv_ref, sems,
):
    lanes = pl.ds(BAND, BAND)
    copies = begin(
        [
            (tok_hbm, tok_ref),
            (wq_hbm.at[:, lanes], wq_ref),
            (wk_hbm.at[:, lanes], wk_ref),
            (wv_hbm.at[:, lanes], wv_ref),
        ],
        sems,
    )
    copies[0].wait()
    tok = jnp.concatenate([to_halves(tok_ref[...]), to_halves(prev_ref[...])], axis=0)
    copies[1].wait()
    q_ref[...] = dot(tok, wq_ref[...]).astype(BF)
    copies[2].wait()
    k_ref[...] = dot(tok, wk_ref[...]).astype(BF)
    copies[3].wait()
    v_ref[...] = dot(tok, wv_ref[...]).astype(BF)


def win_proj(tok, prev, wq, wk, wv):
    return call(
        win_proj_kernel,
        [out_block((2 * TOK, BAND), BF)] * 3,
        12 * TOK * WIDTH * BAND,
        4 * 1024 * 1024,
        [in_vmem(prev)] + [in_hbm(x) for x in (tok, wq, wk, wv)],
        [pltpu.VMEM((TOK, WIDTH), BF)] + [WEIGHT_HALF] * 3 + [pltpu.SemaphoreType.DMA((4,))],
    )


def window_distance(pos):
    key = lax.broadcasted_iota(jnp.int32, (288, 96), 0)
    query = lax.broadcasted_iota(jnp.int32, (288, 96), 1)
    block = (key >= 96).astype(jnp.int32) + (key >= 192).astype(jnp.int32)
    inner = key - 96 * block
    shift = jnp.where(block == 1, -2, jnp.where(block == 2, 2, 0))
    offset = shift + ((inner >> 4) & 1) - ((query >> 4) & 1)
    allowed = (inner & 15) == (query & 15)
    allowed = allowed & ((block != 1) | (pos > 0)) & ((block != 2) | (pos < N_LAT - 1))
    return jnp.where(allowed, jnp.abs(offset), 99)


def extended(two, nxt, half):
    rows = slice(96 * half, 96 * half + 96)
    prows = slice(TOK + 96 * half, TOK + 96 * half + 96)
    return jnp.concatenate([two[rows], two[prows], nxt[rows]], axis=0)


def win_fwd_kernel(
    pos_ref, reach_ref, next_ref, wk_hbm, wv_hbm, wq_hbm, q_hbm, k_hbm, v_hbm,
    o_ref, stat_ref, hq_hbm, hk_hbm, hv_hbm,
    hq_ref, hk_ref, hv_ref, wk_ref, wv_ref, wq_ref, q_ref, k_ref, v_ref, sems, out_sems,
):
    lanes = pl.ds(BAND, BAND)
    copies = begin(
        [
            (wk_hbm.at[:, lanes], wk_ref),
            (wv_hbm.at[:, lanes], wv_ref),
            (wq_hbm.at[:, lanes], wq_ref),
            (q_hbm, q_ref),
            (k_hbm, k_ref),
            (v_hbm, v_ref),
        ],
        sems,
    )
    dist = window_distance(pos_ref[0:1, 0:1])
    near = to_halves(next_ref[...])
    copies[0].wait()
    hk_ref[...] = dot(near, wk_ref[...]).astype(BF)
    copies[1].wait()
    hv_ref[...] = dot(near, wv_ref[...]).astype(BF)
    copies[2].wait()
    hq_ref[...] = dot(near, wq_ref[...]).astype(BF)
    stores = begin([(hk_ref, hk_hbm), (hv_ref, hv_hbm), (hq_ref, hq_hbm)], out_sems)
    for copy in copies[3:6]:
        copy.wait()
    for half in range(2):
        rows = slice(96 * half, 96 * half + 96)
        q = q_ref[rows]
        k = extended(k_ref[...], hk_ref[...], half)
        vt = tr(extended(v_ref[...], hv_ref[...], half))
        outs = []
        tops = []
        rtots = []
        for h in range(HALF):
            lanes = slice(64 * h, 64 * h + 64)
            s = dot_nt(k[:, lanes], q[:, lanes]) * (SCALE * LOG2E)
            s = jnp.where(dist <= reach_ref[h : h + 1, 0:1], s, NEG)
            top = jnp.max(s, axis=0, keepdims=True)
            e = jnp.exp2(s - top)
            rtot = 1.0 / jnp.sum(e, axis=0, keepdims=True)
            w = (e * rtot).astype(BF)
            outs.append(dot(vt[lanes], w))
            tops.append(top)
            rtots.append(rtot)
        o_ref[rows] = tr(jnp.concatenate(outs, axis=0)).astype(BF)
        stats = jnp.concatenate(tops + rtots + [jnp.zeros((112, 96), F32)], axis=0)
        stat_ref[rows] = tr(stats)
    for store in stores:
        store.wait()

def win_fwd(pos, reach, q, k, v, nxt, wq, wk, wv):
    return call(
        win_fwd_kernel,
        [
            out_block((TOK, BAND), BF),
            out_block((TOK, 128), F32),
            out_hbm((TOK, BAND), BF),
            out_hbm((TOK, BAND), BF),
            out_hbm((TOK, BAND), BF),
        ],
        64 * 288 * 128 * 64 + 6 * TOK * WIDTH * BAND,
        6 * 1024 * 1024,
        [in_vmem(pos), in_vmem(reach)]
        + [in_vmem(nxt)]
        + [in_hbm(x) for x in (wk, wv, wq, q, k, v)],
        [pltpu.VMEM((TOK, BAND), BF)] * 3
        + [WEIGHT_HALF] * 3
        + [pltpu.VMEM((2 * TOK, BAND), BF)] * 3
        + [pltpu.SemaphoreType.DMA((6,)), pltpu.SemaphoreType.DMA((3,))],
    )


def statistics(rows):
    parts = tr(rows.astype(F32))
    return parts[0:32] + parts[32:64] + parts[64:96]


def neighbour_distance(pos):
    key = lax.broadcasted_iota(jnp.int32, (96, 192), 0)
    lane = lax.broadcasted_iota(jnp.int32, (96, 192), 1)
    after = lane >= 96
    query = lane - jnp.where(after, 96, 0)
    offset = ((key >> 4) & 1) - ((query >> 4) & 1) + jnp.where(after, -2, 2)
    allowed = (key & 15) == (query & 15)
    allowed = allowed & (after | (pos > 0)) & (~after | (pos < N_LAT - 1))
    return jnp.where(allowed, jnp.abs(offset), 99)


def win_grad_kernel(
    pos_ref, reach_ref, prev_ref, next_ref, q_hbm, k_hbm, v_hbm, hk_hbm, hv_hbm, pay_hbm, hq_hbm,
    dm_hbm, wq_hbm, wk_hbm, wv_hbm, out_ref,
    q_ref, k_ref, v_ref, hk_ref, hv_ref, pay_ref, hq_ref, dm_ref, wq_ref, wk_ref, wv_ref,
    dq_s, dk_s, dv_s, sems,
):
    window = pl.ds(BAND, BAND)
    copies = begin(
        [
            (q_hbm, q_ref),
            (k_hbm, k_ref),
            (v_hbm, v_ref),
            (hk_hbm, hk_ref),
            (hv_hbm, hv_ref),
            (pay_hbm, pay_ref),
            (hq_hbm, hq_ref),
            (wq_hbm.at[:, window], wq_ref),
            (wk_hbm.at[:, window], wk_ref),
            (wv_hbm.at[:, window], wv_ref),
            (dm_hbm, dm_ref),
        ],
        sems,
    )
    dist = window_distance(pos_ref[0:1, 0:1])
    near_dist = neighbour_distance(pos_ref[0:1, 0:1])
    for copy in copies[:7]:
        copy.wait()
    for half in range(2):
        rows = slice(96 * half, 96 * half + 96)
        prows = slice(TOK + 96 * half, TOK + 96 * half + 96)
        q = q_ref[rows]
        k = extended(k_ref[...], hk_ref[...], half)
        v = extended(v_ref[...], hv_ref[...], half)
        kt = tr(k)
        do = pay_ref[rows, 0:BAND]
        stat = statistics(pay_ref[rows, BAND:])
        near_q = jnp.concatenate([q_ref[prows], hq_ref[rows]], axis=0)
        near_pay = jnp.concatenate([prev_ref[rows], next_ref[rows]], axis=0)
        near_do = near_pay[:, 0:BAND]
        near_stat = statistics(near_pay[:, BAND:])
        dqs = []
        for pair in range(HALF // 2):
            dks = []
            dvs = []
            for h in (2 * pair, 2 * pair + 1):
                lanes = slice(64 * h, 64 * h + 64)
                qh, kh, vh, doh = q[:, lanes], k[:, lanes], v[:, lanes], do[:, lanes]
                s = dot_nt(kh, qh) * (SCALE * LOG2E)
                e = jnp.exp2(s - stat[h : h + 1])
                p = jnp.where(dist <= reach_ref[h : h + 1, 0:1], e * stat[8 + h : 9 + h], 0.0)
                dp = dot_nt(vh, doh)
                ds = (p * (dp - stat[16 + h : 17 + h]) * SCALE).astype(BF)
                dqs.append(dot(kt[lanes], ds))
                qn, don = near_q[:, lanes], near_do[:, lanes]
                s = dot_nt(kh[0:96], qn) * (SCALE * LOG2E)
                e = jnp.exp2(s - near_stat[h : h + 1])
                pn = jnp.where(near_dist <= reach_ref[h : h + 1, 0:1], e * near_stat[8 + h : 9 + h], 0.0)
                dp = dot_nt(vh[0:96], don)
                dsn = (pn * (dp - near_stat[16 + h : 17 + h]) * SCALE).astype(BF)
                dvs.append(dot(p[0:96].astype(BF), doh) + dot(pn.astype(BF), don))
                dks.append(dot(ds[0:96], qh) + dot(dsn, qn))
            out = slice(128 * pair, 128 * pair + 128)
            dk_s[rows, out] = jnp.concatenate(dks, axis=1).astype(BF)
            dv_s[rows, out] = jnp.concatenate(dvs, axis=1).astype(BF)
        dq_s[rows] = tr(jnp.concatenate(dqs, axis=0)).astype(BF)
    for copy in copies[7:]:
        copy.wait()
    g = dot_nt(dq_s[...], wq_ref[...])
    g = g + dot_nt(dk_s[...], wk_ref[...]) + dot_nt(dv_s[...], wv_ref[...])
    out_ref[...] = dm_ref[...].astype(F32) + from_halves(g)


def win_grad(pos, reach, q, k, v, hk, hv, pay, hq, prev, nxt, dm, wq, wk, wv):
    return call(
        win_grad_kernel,
        [out_block((TOK, WIDTH), F32)],
        6 * TOK * WIDTH * BAND + 200 * 288 * 128 * 64,
        8 * 1024 * 1024,
        [in_vmem(pos), in_vmem(reach)]
        + [in_vmem(prev), in_vmem(nxt)]
        + [in_hbm(x) for x in (q, k, v, hk, hv, pay, hq, dm, wq, wk, wv)],
        [pltpu.VMEM((2 * TOK, BAND), BF)] * 3
        + [
            pltpu.VMEM((TOK, BAND), BF),
            pltpu.VMEM((TOK, BAND), BF),
            pltpu.VMEM((TOK, BAND + 128), BF),
            pltpu.VMEM((TOK, BAND), BF),
            pltpu.VMEM((TOK, WIDTH), BF),
        ]
        + [WEIGHT_HALF] * 3
        + [pltpu.VMEM((TOK, BAND), BF)] * 3
        + [pltpu.SemaphoreType.DMA((11,))],
    )[0]


def mid_kernel(
    table_ref, tok_hbm, tgt_hbm, win_hbm, stat_hbm, wo_ref, o_ref,
    mixed_hbm, dm_hbm, send_ref, pay_ref, sum_ref,
    tok_ref, tgt_ref, win_ref, stat_ref, mixed_ref, dm_ref, att_s, sems,
):
    copies = begin(
        [(win_hbm, win_ref), (tok_hbm, tok_ref), (tgt_hbm, tgt_ref), (stat_hbm, stat_ref)], sems
    )
    for pair in range(HALF // 2):
        lanes = slice(128 * pair, 128 * pair + 128)
        for l in range(LEVELS):
            for r in range(2):
                base = 64 * l + 32 * r
                a = o_ref[4 * pair + r, 16 * l : 16 * l + 16, :]
                b = o_ref[4 * pair + 2 + r, 16 * l : 16 * l + 16, :]
                att_s[base : base + 16, lanes] = jnp.concatenate([a[:, 0:64], b[:, 0:64]], axis=1)
                att_s[base + 16 : base + 32, lanes] = jnp.concatenate(
                    [a[:, 64:128], b[:, 64:128]], axis=1
                )
    copies[0].wait()
    att_s[:, BAND:] = from_halves(win_ref[...])
    att = att_s[...]
    for copy in copies[1:]:
        copy.wait()
    d_att = jnp.zeros((TOK, WIDTH), F32)
    total = jnp.zeros((8, 256), F32)
    for g in range(4):
        lanes = slice(256 * g, 256 * g + 256)
        mixed = (tok_ref[:, lanes].astype(F32) + dot(att, wo_ref[:, lanes])).astype(BF)
        mixed_ref[:, lanes] = mixed
        diff = mixed.astype(F32) - tgt_ref[:, lanes].astype(F32)
        weighted = (table_ref[g : g + 1, 0:1].astype(F32) * 0.25) * diff
        total = total + jnp.sum((weighted * diff).reshape(TOK // 8, 8, 256), axis=0)
        dm = weighted.astype(BF)
        dm_ref[:, lanes] = dm
        d_att = d_att + dot_nt(dm, wo_ref[:, lanes])
    copies = begin([(mixed_ref, mixed_hbm), (dm_ref, dm_hbm)], sems)
    d_att = d_att.astype(BF)
    dwin = to_halves(d_att[:, BAND:])
    pay_ref[:, 0:BAND] = dwin
    terms = dwin.astype(F32) * win_ref[...].astype(F32)
    first = terms.astype(BF)
    second = (terms - first.astype(F32)).astype(BF)
    feature = lax.broadcasted_iota(jnp.int32, (BAND, 128), 0)
    lane = lax.broadcasted_iota(jnp.int32, (BAND, 128), 1)
    gather = ((feature >> 6) + 16 == lane).astype(F32).astype(BF)
    stat = stat_ref[...] + dot(first, gather) + dot(second, gather)
    high = stat.astype(BF).astype(F32)
    middle = (stat - high).astype(BF).astype(F32)
    low = stat - high - middle
    packed = high + pltpu.roll(middle, 32, 1) + pltpu.roll(low, 64, 1)
    pay_ref[:, BAND:] = packed.astype(BF)
    for h in range(HALF):
        dh = d_att[:, 64 * h : 64 * h + 64]
        for l in range(LEVELS):
            for r in range(2):
                base = 64 * l + 32 * r
                send_ref[2 * h + r, 16 * l : 16 * l + 16, :] = jnp.concatenate(
                    [dh[base : base + 16], dh[base + 16 : base + 32]], axis=1
                )
    sum_ref[...] = jnp.broadcast_to(jnp.sum(total), (8, 128))
    for copy in copies:
        copy.wait()


def mid(table, tok, tgt, o, win, stat, wo):
    return call(
        mid_kernel,
        [
            out_hbm((TOK, WIDTH), BF),
            out_hbm((TOK, WIDTH), BF),
            out_block((N_LON, 48, 128), BF),
            out_block((TOK, BAND + 128), BF),
            out_block((8, 128), F32),
        ],
        4 * TOK * WIDTH * WIDTH,
        4 * 1024 * 1024,
        [in_vmem(table)]
        + [in_hbm(x) for x in (tok, tgt, win, stat)]
        + [in_vmem(x) for x in (wo, o)],
        [pltpu.VMEM((TOK, WIDTH), BF)] * 2
        + [pltpu.VMEM((TOK, BAND), BF), pltpu.VMEM((TOK, 128), F32)]
        + [pltpu.VMEM((TOK, WIDTH), BF)] * 3
        + [pltpu.SemaphoreType.DMA((4,))],
    )


def band_grad_kernel(
    x_ref, base_hbm, wq_hbm, wk_hbm, wv_hbm, out_hbm, loss_ref,
    base_ref, wq_ref, wk_ref, wv_ref, dq_s, dk_s, dv_s, out_s, sems,
):
    band = pl.ds(0, BAND)
    loads = begin(
        [
            (wq_hbm.at[:, band], wq_ref),
            (wk_hbm.at[:, band], wk_ref),
            (wv_hbm.at[:, band], wv_ref),
            (base_hbm, base_ref),
        ],
        sems,
    )
    for pair in range(HALF // 2):
        lanes = slice(128 * pair, 128 * pair + 128)
        for l in range(LEVELS):
            for r in range(2):
                base = 64 * l + 32 * r
                a = x_ref[4 * pair + r, 48 * l : 48 * l + 48, :]
                b = x_ref[4 * pair + 2 + r, 48 * l : 48 * l + 48, :]
                first = jnp.concatenate([a[:, 0:64], b[:, 0:64]], axis=1)
                second = jnp.concatenate([a[:, 64:128], b[:, 64:128]], axis=1)
                dq_s[base : base + 32, lanes] = first[0:32]
                dk_s[base : base + 32, lanes] = second[0:32]
                dv_s[base : base + 16, lanes] = first[32:48]
                dv_s[base + 16 : base + 32, lanes] = second[32:48]
    dq = dq_s[...]
    dk = dk_s[...]
    dv = dv_s[...]
    loads[0].wait()
    out_s[...] = dot_nt(dq, wq_ref[...])
    loads[1].wait()
    out_s[...] += dot_nt(dk, wk_ref[...])
    loads[2].wait()
    loads[3].wait()
    copies = []
    for n in range(4):
        rows = slice(256 * n, 256 * n + 256)
        out_s[:, rows] += base_ref[:, rows] + dot_nt(dv, wv_ref[rows, :])
        lanes = pl.ds(256 * n, 256)
        copy = pltpu.make_async_copy(out_s.at[:, lanes], out_hbm.at[:, lanes], sems.at[n])
        copy.start()
        copies.append(copy)
    loss_ref[0, 0] = jnp.sum(x_ref[:, 144, :].astype(F32)) * (1.0 / 25165824)
    for copy in copies:
        copy.wait()


def band_grad(x, base, wq, wk, wv):
    return call(
        band_grad_kernel,
        [
            out_hbm((TOK, WIDTH), F32),
            (pl.BlockSpec(memory_space=pltpu.SMEM), jax.ShapeDtypeStruct((1, 1), F32)),
        ],
        6 * TOK * WIDTH * BAND,
        5 * 1024 * 1024,
        [in_vmem(x)] + [in_hbm(y) for y in (base, wq, wk, wv)],
        [pltpu.VMEM((TOK, WIDTH), F32)]
        + [WEIGHT_HALF] * 3
        + [pltpu.VMEM((TOK, BAND), BF)] * 3
        + [pltpu.VMEM((TOK, WIDTH), F32), pltpu.SemaphoreType.DMA((4,))],
    )


def swap(x):
    return lax.all_to_all(x, "lon", 0, 0, tiled=True)


UP = [(i, (i + 1) % N_LAT) for i in range(N_LAT)]
DOWN = [((i + 1) % N_LAT, i) for i in range(N_LAT)]


def per_device(tokens, targets, w_query, w_key, w_value, w_out, window_reach, loss_table):
    levels, rows, cols, width = tokens.shape
    count = levels * rows * cols
    tok = tokens.reshape(count, width)
    tgt = targets.reshape(count, width)
    pos = jnp.broadcast_to(lax.axis_index("lat").astype(jnp.int32), (8, 128))
    window_reach = jnp.broadcast_to(window_reach[:, None], (8, 128))
    loss_table = jnp.broadcast_to(jnp.tile(loss_table, 2)[:, None], (8, 128))
    with jax.named_scope("band_projection"):
        sent = band_proj(tok, w_query, w_key, w_value)
    with jax.named_scope("halo_tokens"):
        prev = lax.ppermute(tok, "lat", UP)
    with jax.named_scope("band_qkv_exchange"):
        x = swap(sent)
    with jax.named_scope("window_projection"):
        q, k, v = win_proj(tok, prev, w_query, w_key, w_value)
        x, q, k, v, tok_later = lax.optimization_barrier((x, q, k, v, tok))
        nxt = lax.ppermute(tok_later, "lat", DOWN)
    with jax.named_scope("band_forward"):
        o, stat = band_fwd(x)
        o_back = swap(o)
    with jax.named_scope("window_forward"):
        win, wstat, hq, hk, hv = win_fwd(
            pos, window_reach, q, k, v, nxt, w_query, w_key, w_value
        )
    with jax.named_scope("middle"):
        mixed, dm, dsend, pay, part = mid(loss_table, tok, tgt, o_back, win, wstat, w_out)
        do = swap(dsend)
        pay_next = lax.ppermute(pay, "lat", DOWN)
        pay_prev = lax.ppermute(pay, "lat", UP)
        losses = [part] + [
            lax.ppermute(part, "lat", [(i, i ^ step) for i in range(N_LAT)]) for step in (1, 2, 3)
        ]
    with jax.named_scope("band_backward"):
        four = losses[0] + losses[1] + losses[2] + losses[3]
        far = lax.ppermute(four, "lat", [(i, i ^ 4) for i in range(N_LAT)])
        dsent = band_bwd(x, o, stat, do, four, far)
        dx = swap(dsent)
    with jax.named_scope("window_gradient"):
        base = win_grad(
            pos, window_reach, q, k, v, hk, hv, pay, hq, pay_prev, pay_next, dm,
            w_query, w_key, w_value,
        )
    with jax.named_scope("token_gradient"):
        grad, loss = band_grad(dx, base, w_query, w_key, w_value)
    full = (levels, rows, cols, width)
    return (mixed.reshape(full), grad.reshape(full), loss.reshape(()))


def solution(mesh):
    spec = P(None, "lat", "lon", None)
    return jax.shard_map(
        per_device,
        mesh=mesh,
        in_specs=(spec, spec, P(), P(), P(), P(), P(), P()),
        out_specs=(spec, spec, P()),
        check_vma=False,
    )
```

```python
import functools
import math

import jax
import jax.numpy as jnp
from jax import lax
from jax.experimental import pallas as pl
from jax.experimental.pallas import tpu as pltpu
from jax.sharding import PartitionSpec as P

HEADS = 16
HALF = 8
HD = 64
LEVELS = 3
N_LON = 16
N_LAT = 8
TOK = 192
WIDTH = 1024
BAND = 512
SCALE = 0.125
LOG2E = math.log2(math.e)
NEG = -1e30
BF = jnp.bfloat16
F32 = jnp.float32
VMEM = 32 * 1024 * 1024


def call(kernel, outs, flops, nbytes, ins, scratch=()):
    return pl.pallas_call(
        kernel,
        grid=(1,),
        in_specs=[spec for spec, _ in ins],
        out_specs=tuple(spec for spec, _ in outs),
        out_shape=tuple(shape for _, shape in outs),
        scratch_shapes=list(scratch),
        compiler_params=pltpu.CompilerParams(vmem_limit_bytes=VMEM),
        cost_estimate=pl.CostEstimate(flops=50 * flops, bytes_accessed=nbytes, transcendentals=0),
    )(*[x for _, x in ins])


def in_smem(x):
    return (pl.BlockSpec(memory_space=pltpu.SMEM), x)


def in_vmem(x):
    return (pl.BlockSpec(memory_space=pltpu.VMEM), x)


def in_hbm(x):
    return (pl.BlockSpec(memory_space=pltpu.HBM), hbm(x))


def out_vmem(shape, dtype):
    return (pl.BlockSpec(memory_space=pltpu.VMEM), pltpu.VMEM(shape, dtype))


def out_hbm(shape, dtype):
    return (pl.BlockSpec(memory_space=pltpu.HBM), pltpu.HBM(shape, dtype))


def out_block(shape, dtype):
    zeros = (0,) * len(shape)
    return (pl.BlockSpec(shape, lambda g: zeros), pltpu.HBM(shape, dtype))


def begin(pairs, sems):
    copies = [pltpu.make_async_copy(a, b, sems.at[n]) for n, (a, b) in enumerate(pairs)]
    for copy in copies:
        copy.start()
    return copies


def hbm(x):
    return pltpu.with_memory_space_constraint(x, pltpu.HBM)


def dot(a, b):
    return jnp.dot(a, b, preferred_element_type=F32)


def dot_nt(a, b):
    return lax.dot_general(a, b, (((1,), (1,)), ((), ())), preferred_element_type=F32)


def tr(x):
    return jnp.transpose(x)


def band_proj_kernel(
    tok_hbm, wq_hbm, wk_hbm, wv_hbm, out_ref, tok_ref, wq_ref, wk_ref, wv_ref, sems
):
    lanes = pl.ds(0, BAND)
    copies = begin(
        [
            (tok_hbm, tok_ref),
            (wq_hbm.at[:, lanes], wq_ref),
            (wk_hbm.at[:, lanes], wk_ref),
            (wv_hbm.at[:, lanes], wv_ref),
        ],
        sems,
    )
    copies[0].wait()
    tok = tok_ref[...]
    copies[1].wait()
    q = dot(tok, wq_ref[...]).astype(BF)
    copies[2].wait()
    k = dot(tok, wk_ref[...]).astype(BF)
    copies[3].wait()
    v = dot(tok, wv_ref[...]).astype(BF)
    for h in range(HALF):
        lanes = slice(64 * h, 64 * h + 64)
        qk = jnp.concatenate([q[:, lanes], k[:, lanes]], axis=1)
        vh = v[:, lanes]
        for l in range(LEVELS):
            for r in range(2):
                base = l * 64 + r * 32
                out_ref[2 * h + r, 48 * l : 48 * l + 32, :] = qk[base : base + 32]
                out_ref[2 * h + r, 48 * l + 32 : 48 * l + 48, :] = jnp.concatenate(
                    [vh[base : base + 16], vh[base + 16 : base + 32]], axis=1
                )


WEIGHT_HALF = pltpu.VMEM((WIDTH, BAND), BF)


def band_proj(tok, wq, wk, wv):
    return call(
        band_proj_kernel,
        [out_block((N_LON, 144, 128), BF)],
        6 * TOK * WIDTH * BAND,
        4 * 1024 * 1024,
        [in_hbm(x) for x in (tok, wq, wk, wv)],
        [pltpu.VMEM((TOK, WIDTH), BF)] + [WEIGHT_HALF] * 3 + [pltpu.SemaphoreType.DMA((4,))],
    )[0]


def unpack_qkv(x):
    qk = x[:, 0:32, :].reshape(512, 128)
    v = x[:, 32:48, :]
    v = jnp.concatenate([v[:, :, 0:64], v[:, :, 64:128]], axis=1).reshape(512, 64)
    return qk[:, 0:64], qk[:, 64:128], v


def unpack_one(x):
    return jnp.concatenate([x[:, :, 0:64], x[:, :, 64:128]], axis=1).reshape(512, 64)


def pack_one(x):
    x = x.reshape(N_LON, 32, 64)
    return jnp.concatenate([x[:, 0:16, :], x[:, 16:32, :]], axis=2)


def band_fwd_kernel(x_ref, o_hbm, stat_ref, o_ref, sems):
    stores = []
    for l in range(LEVELS):
        q, k, v = unpack_qkv(x_ref[:, 48 * l : 48 * l + 48, :])
        s = dot_nt(k, q) * (SCALE * LOG2E)
        top = jnp.max(s, axis=0, keepdims=True)
        e = jnp.exp2(s - top)
        rtot = 1.0 / jnp.sum(e, axis=0, keepdims=True)
        w = (e * rtot).astype(BF)
        o = tr(dot(tr(v), w)).astype(BF)
        o_ref[:, 16 * l : 16 * l + 16, :] = pack_one(o)
        stat_ref[l, 0:1, :] = top
        stat_ref[l, 1:2, :] = rtot
        rows = pl.ds(16 * l, 16)
        stores += begin([(o_ref.at[:, rows], o_hbm.at[:, rows])], sems.at[pl.ds(l, 1)])
    for store in stores:
        store.wait()


def band_fwd(x):
    return call(
        band_fwd_kernel,
        [out_hbm((N_LON, 48, 128), BF), out_vmem((LEVELS, 2, 512), F32)],
        12 * 512 * 512 * 64,
        1024 * 1024,
        [in_vmem(x)],
        [pltpu.VMEM((N_LON, 48, 128), BF), pltpu.SemaphoreType.DMA((3,))],
    )


def band_bwd_kernel(x_ref, o_ref, stat_ref, do_ref, mine_ref, other_ref, out_hbm, out_ref, sems):
    total = jnp.broadcast_to(mine_ref[0:1, :] + other_ref[0:1, :], (16, 128))
    high = total.astype(BF).astype(F32)
    mid = (total - high).astype(BF).astype(F32)
    low = total - high - mid
    at = lax.broadcasted_iota(jnp.int32, (16, 128), 1)
    parts = jnp.where(at == 0, high, jnp.where(at == 1, mid, jnp.where(at == 2, low, 0.0)))
    parts = parts.astype(BF)
    for j in range(N_LON):
        out_ref[j, 144:160, :] = parts
    rows = pl.ds(144, 16)
    stores = begin([(out_ref.at[:, rows], out_hbm.at[:, rows])], sems.at[pl.ds(3, 1)])
    for l in range(LEVELS):
        q, k, v = unpack_qkv(x_ref[:, 48 * l : 48 * l + 48, :])
        o = unpack_one(o_ref[:, 16 * l : 16 * l + 16, :])
        do = unpack_one(do_ref[:, 16 * l : 16 * l + 16, :])
        s = dot_nt(k, q) * (SCALE * LOG2E)
        p = jnp.exp2(s - stat_ref[l, 0:1, :]) * stat_ref[l, 1:2, :]
        w = p.astype(BF)
        dp = dot_nt(v, do)
        delta = jnp.sum(tr(do.astype(F32) * o.astype(F32)), axis=0, keepdims=True)
        ds = (p * (dp - delta) * SCALE).astype(BF)
        dv = dot(w, do).astype(BF)
        dk = dot(ds, q).astype(BF)
        dq = tr(dot(tr(k), ds)).astype(BF)
        out_ref[:, 48 * l : 48 * l + 32, :] = jnp.concatenate([dq, dk], axis=1).reshape(
            N_LON, 32, 128
        )
        out_ref[:, 48 * l + 32 : 48 * l + 48, :] = pack_one(dv)
        rows = pl.ds(48 * l, 48)
        stores += begin([(out_ref.at[:, rows], out_hbm.at[:, rows])], sems.at[pl.ds(l, 1)])
    for store in stores:
        store.wait()


def band_bwd(x, o, stat, do, mine, other):
    return call(
        band_bwd_kernel,
        [out_hbm((N_LON, 160, 128), BF)],
        30 * 512 * 512 * 64,
        2 * 1024 * 1024,
        [in_vmem(y) for y in (x, o, stat, do, mine, other)],
        [pltpu.VMEM((N_LON, 160, 128), BF), pltpu.SemaphoreType.DMA((4,))],
    )[0]


def to_halves(x):
    return jnp.concatenate(
        [x[32 * i + 16 * s : 32 * i + 16 * s + 16] for s in range(2) for i in range(6)], axis=0
    )


def from_halves(x):
    return jnp.concatenate(
        [x[96 * s + 16 * i : 96 * s + 16 * i + 16] for i in range(6) for s in range(2)], axis=0
    )


def win_proj_kernel(
    prev_ref, tok_hbm, wq_hbm, wk_hbm, wv_hbm, q_ref, k_ref, v_ref,
    tok_ref, wq_ref, wk_ref, wv_ref, sems,
):
    lanes = pl.ds(BAND, BAND)
    copies = begin(
        [
            (tok_hbm, tok_ref),
            (wq_hbm.at[:, lanes], wq_ref),
            (wk_hbm.at[:, lanes], wk_ref),
            (wv_hbm.at[:, lanes], wv_ref),
        ],
        sems,
    )
    copies[0].wait()
    tok = jnp.concatenate([to_halves(tok_ref[...]), to_halves(prev_ref[...])], axis=0)
    copies[1].wait()
    q_ref[...] = dot(tok, wq_ref[...]).astype(BF)
    copies[2].wait()
    k_ref[...] = dot(tok, wk_ref[...]).astype(BF)
    copies[3].wait()
    v_ref[...] = dot(tok, wv_ref[...]).astype(BF)


def win_proj(tok, prev, wq, wk, wv):
    return call(
        win_proj_kernel,
        [out_block((2 * TOK, BAND), BF)] * 3,
        12 * TOK * WIDTH * BAND,
        4 * 1024 * 1024,
        [in_vmem(prev)] + [in_hbm(x) for x in (tok, wq, wk, wv)],
        [pltpu.VMEM((TOK, WIDTH), BF)] + [WEIGHT_HALF] * 3 + [pltpu.SemaphoreType.DMA((4,))],
    )


def window_distance(pos):
    key = lax.broadcasted_iota(jnp.int32, (288, 96), 0)
    query = lax.broadcasted_iota(jnp.int32, (288, 96), 1)
    block = (key >= 96).astype(jnp.int32) + (key >= 192).astype(jnp.int32)
    inner = key - 96 * block
    shift = jnp.where(block == 1, -2, jnp.where(block == 2, 2, 0))
    offset = shift + ((inner >> 4) & 1) - ((query >> 4) & 1)
    allowed = (inner & 15) == (query & 15)
    allowed = allowed & ((block != 1) | (pos > 0)) & ((block != 2) | (pos < N_LAT - 1))
    return jnp.where(allowed, jnp.abs(offset), 99)


def extended(two, nxt, half):
    rows = slice(96 * half, 96 * half + 96)
    prows = slice(TOK + 96 * half, TOK + 96 * half + 96)
    return jnp.concatenate([two[rows], two[prows], nxt[rows]], axis=0)


def win_fwd_kernel(
    pos_ref, reach_ref, next_ref, wk_hbm, wv_hbm, wq_hbm, q_hbm, k_hbm, v_hbm,
    o_ref, stat_ref, hq_hbm, hk_hbm, hv_hbm,
    hq_ref, hk_ref, hv_ref, wk_ref, wv_ref, wq_ref, q_ref, k_ref, v_ref, sems, out_sems,
):
    lanes = pl.ds(BAND, BAND)
    copies = begin(
        [
            (wk_hbm.at[:, lanes], wk_ref),
            (wv_hbm.at[:, lanes], wv_ref),
            (wq_hbm.at[:, lanes], wq_ref),
            (q_hbm, q_ref),
            (k_hbm, k_ref),
            (v_hbm, v_ref),
        ],
        sems,
    )
    dist = window_distance(pos_ref[0:1, 0:1])
    near = to_halves(next_ref[...])
    copies[0].wait()
    hk_ref[...] = dot(near, wk_ref[...]).astype(BF)
    copies[1].wait()
    hv_ref[...] = dot(near, wv_ref[...]).astype(BF)
    copies[2].wait()
    hq_ref[...] = dot(near, wq_ref[...]).astype(BF)
    stores = begin([(hk_ref, hk_hbm), (hv_ref, hv_hbm), (hq_ref, hq_hbm)], out_sems)
    for copy in copies[3:6]:
        copy.wait()
    for half in range(2):
        rows = slice(96 * half, 96 * half + 96)
        q = q_ref[rows]
        k = extended(k_ref[...], hk_ref[...], half)
        vt = tr(extended(v_ref[...], hv_ref[...], half))
        outs = []
        tops = []
        rtots = []
        for h in range(HALF):
            lanes = slice(64 * h, 64 * h + 64)
            s = dot_nt(k[:, lanes], q[:, lanes]) * (SCALE * LOG2E)
            s = jnp.where(dist <= reach_ref[h : h + 1, 0:1], s, NEG)
            top = jnp.max(s, axis=0, keepdims=True)
            e = jnp.exp2(s - top)
            rtot = 1.0 / jnp.sum(e, axis=0, keepdims=True)
            w = (e * rtot).astype(BF)
            outs.append(dot(vt[lanes], w))
            tops.append(top)
            rtots.append(rtot)
        o_ref[rows] = tr(jnp.concatenate(outs, axis=0)).astype(BF)
        stats = jnp.concatenate(tops + rtots + [jnp.zeros((112, 96), F32)], axis=0)
        stat_ref[rows] = tr(stats)
    for store in stores:
        store.wait()

def win_fwd(pos, reach, q, k, v, nxt, wq, wk, wv):
    return call(
        win_fwd_kernel,
        [
            out_block((TOK, BAND), BF),
            out_block((TOK, 128), F32),
            out_hbm((TOK, BAND), BF),
            out_hbm((TOK, BAND), BF),
            out_hbm((TOK, BAND), BF),
        ],
        64 * 288 * 128 * 64 + 6 * TOK * WIDTH * BAND,
        6 * 1024 * 1024,
        [in_vmem(pos), in_vmem(reach)]
        + [in_vmem(nxt)]
        + [in_hbm(x) for x in (wk, wv, wq, q, k, v)],
        [pltpu.VMEM((TOK, BAND), BF)] * 3
        + [WEIGHT_HALF] * 3
        + [pltpu.VMEM((2 * TOK, BAND), BF)] * 3
        + [pltpu.SemaphoreType.DMA((6,)), pltpu.SemaphoreType.DMA((3,))],
    )


def statistics(rows):
    parts = tr(rows.astype(F32))
    return parts[0:32] + parts[32:64] + parts[64:96]


def neighbour_distance(pos):
    key = lax.broadcasted_iota(jnp.int32, (96, 192), 0)
    lane = lax.broadcasted_iota(jnp.int32, (96, 192), 1)
    after = lane >= 96
    query = lane - jnp.where(after, 96, 0)
    offset = ((key >> 4) & 1) - ((query >> 4) & 1) + jnp.where(after, -2, 2)
    allowed = (key & 15) == (query & 15)
    allowed = allowed & (after | (pos > 0)) & (~after | (pos < N_LAT - 1))
    return jnp.where(allowed, jnp.abs(offset), 99)


def win_grad_kernel(
    pos_ref, reach_ref, prev_ref, next_ref, q_hbm, k_hbm, v_hbm, hk_hbm, hv_hbm, pay_hbm, hq_hbm,
    dm_hbm, wq_hbm, wk_hbm, wv_hbm, out_ref,
    q_ref, k_ref, v_ref, hk_ref, hv_ref, pay_ref, hq_ref, dm_ref, wq_ref, wk_ref, wv_ref,
    dq_s, dk_s, dv_s, sems,
):
    window = pl.ds(BAND, BAND)
    copies = begin(
        [
            (q_hbm, q_ref),
            (k_hbm, k_ref),
            (v_hbm, v_ref),
            (hk_hbm, hk_ref),
            (hv_hbm, hv_ref),
            (pay_hbm, pay_ref),
            (hq_hbm, hq_ref),
            (wq_hbm.at[:, window], wq_ref),
            (wk_hbm.at[:, window], wk_ref),
            (wv_hbm.at[:, window], wv_ref),
            (dm_hbm, dm_ref),
        ],
        sems,
    )
    dist = window_distance(pos_ref[0:1, 0:1])
    near_dist = neighbour_distance(pos_ref[0:1, 0:1])
    for copy in copies[:7]:
        copy.wait()
    for half in range(2):
        rows = slice(96 * half, 96 * half + 96)
        prows = slice(TOK + 96 * half, TOK + 96 * half + 96)
        q = q_ref[rows]
        k = extended(k_ref[...], hk_ref[...], half)
        v = extended(v_ref[...], hv_ref[...], half)
        kt = tr(k)
        do = pay_ref[rows, 0:BAND]
        stat = statistics(pay_ref[rows, BAND:])
        near_q = jnp.concatenate([q_ref[prows], hq_ref[rows]], axis=0)
        near_pay = jnp.concatenate([prev_ref[rows], next_ref[rows]], axis=0)
        near_do = near_pay[:, 0:BAND]
        near_stat = statistics(near_pay[:, BAND:])
        dqs = []
        for pair in range(HALF // 2):
            dks = []
            dvs = []
            for h in (2 * pair, 2 * pair + 1):
                lanes = slice(64 * h, 64 * h + 64)
                qh, kh, vh, doh = q[:, lanes], k[:, lanes], v[:, lanes], do[:, lanes]
                s = dot_nt(kh, qh) * (SCALE * LOG2E)
                e = jnp.exp2(s - stat[h : h + 1])
                p = jnp.where(dist <= reach_ref[h : h + 1, 0:1], e * stat[8 + h : 9 + h], 0.0)
                dp = dot_nt(vh, doh)
                ds = (p * (dp - stat[16 + h : 17 + h]) * SCALE).astype(BF)
                dqs.append(dot(kt[lanes], ds))
                qn, don = near_q[:, lanes], near_do[:, lanes]
                s = dot_nt(kh[0:96], qn) * (SCALE * LOG2E)
                e = jnp.exp2(s - near_stat[h : h + 1])
                pn = jnp.where(near_dist <= reach_ref[h : h + 1, 0:1], e * near_stat[8 + h : 9 + h], 0.0)
                dp = dot_nt(vh[0:96], don)
                dsn = (pn * (dp - near_stat[16 + h : 17 + h]) * SCALE).astype(BF)
                dvs.append(dot(p[0:96].astype(BF), doh) + dot(pn.astype(BF), don))
                dks.append(dot(ds[0:96], qh) + dot(dsn, qn))
            out = slice(128 * pair, 128 * pair + 128)
            dk_s[rows, out] = jnp.concatenate(dks, axis=1).astype(BF)
            dv_s[rows, out] = jnp.concatenate(dvs, axis=1).astype(BF)
        dq_s[rows] = tr(jnp.concatenate(dqs, axis=0)).astype(BF)
    for copy in copies[7:]:
        copy.wait()
    g = dot_nt(dq_s[...], wq_ref[...])
    g = g + dot_nt(dk_s[...], wk_ref[...]) + dot_nt(dv_s[...], wv_ref[...])
    out_ref[...] = dm_ref[...].astype(F32) + from_halves(g)


def win_grad(pos, reach, q, k, v, hk, hv, pay, hq, prev, nxt, dm, wq, wk, wv):
    return call(
        win_grad_kernel,
        [out_block((TOK, WIDTH), F32)],
        6 * TOK * WIDTH * BAND + 200 * 288 * 128 * 64,
        8 * 1024 * 1024,
        [in_vmem(pos), in_vmem(reach)]
        + [in_vmem(prev), in_vmem(nxt)]
        + [in_hbm(x) for x in (q, k, v, hk, hv, pay, hq, dm, wq, wk, wv)],
        [pltpu.VMEM((2 * TOK, BAND), BF)] * 3
        + [
            pltpu.VMEM((TOK, BAND), BF),
            pltpu.VMEM((TOK, BAND), BF),
            pltpu.VMEM((TOK, BAND + 128), BF),
            pltpu.VMEM((TOK, BAND), BF),
            pltpu.VMEM((TOK, WIDTH), BF),
        ]
        + [WEIGHT_HALF] * 3
        + [pltpu.VMEM((TOK, BAND), BF)] * 3
        + [pltpu.SemaphoreType.DMA((11,))],
    )[0]


def mid_kernel(
    table_ref, tok_hbm, tgt_hbm, win_hbm, stat_hbm, wo_ref, o_ref,
    mixed_hbm, dm_hbm, send_hbm, pay_ref, sum_ref,
    tok_ref, tgt_ref, win_ref, stat_ref, mixed_ref, dm_ref, att_s, send_ref, sems, send_sems,
):
    copies = begin(
        [(win_hbm, win_ref), (tok_hbm, tok_ref), (tgt_hbm, tgt_ref), (stat_hbm, stat_ref)], sems
    )
    for pair in range(HALF // 2):
        lanes = slice(128 * pair, 128 * pair + 128)
        for l in range(LEVELS):
            for r in range(2):
                base = 64 * l + 32 * r
                a = o_ref[4 * pair + r, 16 * l : 16 * l + 16, :]
                b = o_ref[4 * pair + 2 + r, 16 * l : 16 * l + 16, :]
                att_s[base : base + 16, lanes] = jnp.concatenate([a[:, 0:64], b[:, 0:64]], axis=1)
                att_s[base + 16 : base + 32, lanes] = jnp.concatenate(
                    [a[:, 64:128], b[:, 64:128]], axis=1
                )
    copies[0].wait()
    att_s[:, BAND:] = from_halves(win_ref[...])
    att = att_s[...]
    for copy in copies[1:]:
        copy.wait()
    d_att = jnp.zeros((TOK, WIDTH), F32)
    total = jnp.zeros((8, 256), F32)
    for g in range(4):
        lanes = slice(256 * g, 256 * g + 256)
        mixed = (tok_ref[:, lanes].astype(F32) + dot(att, wo_ref[:, lanes])).astype(BF)
        mixed_ref[:, lanes] = mixed
        diff = mixed.astype(F32) - tgt_ref[:, lanes].astype(F32)
        weighted = (table_ref[g : g + 1, 0:1].astype(F32) * 0.25) * diff
        total = total + jnp.sum((weighted * diff).reshape(TOK // 8, 8, 256), axis=0)
        dm = weighted.astype(BF)
        dm_ref[:, lanes] = dm
        d_att = d_att + dot_nt(dm, wo_ref[:, lanes])
    copies = begin([(mixed_ref, mixed_hbm), (dm_ref, dm_hbm)], sems)
    d_att = d_att.astype(BF)
    for h in range(HALF):
        dh = d_att[:, 64 * h : 64 * h + 64]
        for l in range(LEVELS):
            for r in range(2):
                base = 64 * l + 32 * r
                send_ref[2 * h + r, 16 * l : 16 * l + 16, :] = jnp.concatenate(
                    [dh[base : base + 16], dh[base + 16 : base + 32]], axis=1
                )
    stores = begin([(send_ref, send_hbm)], send_sems)
    dwin = to_halves(d_att[:, BAND:])
    pay_ref[:, 0:BAND] = dwin
    terms = dwin.astype(F32) * win_ref[...].astype(F32)
    first = terms.astype(BF)
    second = (terms - first.astype(F32)).astype(BF)
    feature = lax.broadcasted_iota(jnp.int32, (BAND, 128), 0)
    lane = lax.broadcasted_iota(jnp.int32, (BAND, 128), 1)
    gather = ((feature >> 6) + 16 == lane).astype(F32).astype(BF)
    stat = stat_ref[...] + dot(first, gather) + dot(second, gather)
    high = stat.astype(BF).astype(F32)
    middle = (stat - high).astype(BF).astype(F32)
    low = stat - high - middle
    packed = high + pltpu.roll(middle, 32, 1) + pltpu.roll(low, 64, 1)
    pay_ref[:, BAND:] = packed.astype(BF)
    sum_ref[...] = jnp.broadcast_to(jnp.sum(total), (8, 128))
    for copy in copies + stores:
        copy.wait()


def mid(table, tok, tgt, o, win, stat, wo):
    return call(
        mid_kernel,
        [
            out_hbm((TOK, WIDTH), BF),
            out_hbm((TOK, WIDTH), BF),
            out_hbm((N_LON, 48, 128), BF),
            out_block((TOK, BAND + 128), BF),
            out_block((8, 128), F32),
        ],
        4 * TOK * WIDTH * WIDTH,
        4 * 1024 * 1024,
        [in_vmem(table)]
        + [in_hbm(x) for x in (tok, tgt, win, stat)]
        + [in_vmem(x) for x in (wo, o)],
        [pltpu.VMEM((TOK, WIDTH), BF)] * 2
        + [pltpu.VMEM((TOK, BAND), BF), pltpu.VMEM((TOK, 128), F32)]
        + [pltpu.VMEM((TOK, WIDTH), BF)] * 3
        + [pltpu.VMEM((N_LON, 48, 128), BF)]
        + [pltpu.SemaphoreType.DMA((4,)), pltpu.SemaphoreType.DMA((1,))],
    )


def band_grad_kernel(
    x_ref, base_hbm, wq_hbm, wk_hbm, wv_hbm, out_hbm, loss_ref,
    base_ref, wq_ref, wk_ref, wv_ref, dq_s, dk_s, dv_s, out_s, sems,
):
    band = pl.ds(0, BAND)
    loads = begin(
        [
            (wq_hbm.at[:, band], wq_ref),
            (wk_hbm.at[:, band], wk_ref),
            (wv_hbm.at[:, band], wv_ref),
            (base_hbm, base_ref),
        ],
        sems,
    )
    for pair in range(HALF // 2):
        lanes = slice(128 * pair, 128 * pair + 128)
        for l in range(LEVELS):
            for r in range(2):
                base = 64 * l + 32 * r
                a = x_ref[4 * pair + r, 48 * l : 48 * l + 48, :]
                b = x_ref[4 * pair + 2 + r, 48 * l : 48 * l + 48, :]
                first = jnp.concatenate([a[:, 0:64], b[:, 0:64]], axis=1)
                second = jnp.concatenate([a[:, 64:128], b[:, 64:128]], axis=1)
                dq_s[base : base + 32, lanes] = first[0:32]
                dk_s[base : base + 32, lanes] = second[0:32]
                dv_s[base : base + 16, lanes] = first[32:48]
                dv_s[base + 16 : base + 32, lanes] = second[32:48]
    dq = dq_s[...]
    dk = dk_s[...]
    dv = dv_s[...]
    loads[0].wait()
    out_s[...] = dot_nt(dq, wq_ref[...])
    loads[1].wait()
    out_s[...] += dot_nt(dk, wk_ref[...])
    loads[2].wait()
    loads[3].wait()
    copies = []
    for n in range(4):
        rows = slice(256 * n, 256 * n + 256)
        out_s[:, rows] += base_ref[:, rows] + dot_nt(dv, wv_ref[rows, :])
        lanes = pl.ds(256 * n, 256)
        copy = pltpu.make_async_copy(out_s.at[:, lanes], out_hbm.at[:, lanes], sems.at[n])
        copy.start()
        copies.append(copy)
    loss_ref[0, 0] = jnp.sum(x_ref[:, 144, :].astype(F32)) * (1.0 / 25165824)
    for copy in copies:
        copy.wait()


def band_grad(x, base, wq, wk, wv):
    return call(
        band_grad_kernel,
        [
            out_hbm((TOK, WIDTH), F32),
            (pl.BlockSpec(memory_space=pltpu.SMEM), jax.ShapeDtypeStruct((1, 1), F32)),
        ],
        6 * TOK * WIDTH * BAND,
        5 * 1024 * 1024,
        [in_vmem(x)] + [in_hbm(y) for y in (base, wq, wk, wv)],
        [pltpu.VMEM((TOK, WIDTH), F32)]
        + [WEIGHT_HALF] * 3
        + [pltpu.VMEM((TOK, BAND), BF)] * 3
        + [pltpu.VMEM((TOK, WIDTH), F32), pltpu.SemaphoreType.DMA((4,))],
    )


def swap(x):
    return lax.all_to_all(x, "lon", 0, 0, tiled=True)


UP = [(i, (i + 1) % N_LAT) for i in range(N_LAT)]
DOWN = [((i + 1) % N_LAT, i) for i in range(N_LAT)]


def per_device(tokens, targets, w_query, w_key, w_value, w_out, window_reach, loss_table):
    levels, rows, cols, width = tokens.shape
    count = levels * rows * cols
    tok = tokens.reshape(count, width)
    tgt = targets.reshape(count, width)
    pos = jnp.broadcast_to(lax.axis_index("lat").astype(jnp.int32), (8, 128))
    window_reach = jnp.broadcast_to(window_reach[:, None], (8, 128))
    loss_table = jnp.broadcast_to(jnp.tile(loss_table, 2)[:, None], (8, 128))
    with jax.named_scope("band_projection"):
        sent = band_proj(tok, w_query, w_key, w_value)
    with jax.named_scope("halo_tokens"):
        prev = lax.ppermute(tok, "lat", UP)
    with jax.named_scope("band_qkv_exchange"):
        x = swap(sent)
    with jax.named_scope("window_projection"):
        q, k, v = win_proj(tok, prev, w_query, w_key, w_value)
        x, q, k, v, tok_later = lax.optimization_barrier((x, q, k, v, tok))
        nxt = lax.ppermute(tok_later, "lat", DOWN)
    with jax.named_scope("band_forward"):
        o, stat = band_fwd(x)
        o_back = swap(o)
    with jax.named_scope("window_forward"):
        win, wstat, hq, hk, hv = win_fwd(
            pos, window_reach, q, k, v, nxt, w_query, w_key, w_value
        )
    with jax.named_scope("middle"):
        mixed, dm, dsend, pay, part = mid(loss_table, tok, tgt, o_back, win, wstat, w_out)
        do = swap(dsend)
        pay_next = lax.ppermute(pay, "lat", DOWN)
        pay_prev = lax.ppermute(pay, "lat", UP)
        losses = [part] + [
            lax.ppermute(part, "lat", [(i, i ^ step) for i in range(N_LAT)]) for step in (1, 2, 3)
        ]
    with jax.named_scope("band_backward"):
        four = losses[0] + losses[1] + losses[2] + losses[3]
        far = lax.ppermute(four, "lat", [(i, i ^ 4) for i in range(N_LAT)])
        dsent = band_bwd(x, o, stat, do, four, far)
        dx = swap(dsent)
    with jax.named_scope("window_gradient"):
        base = win_grad(
            pos, window_reach, q, k, v, hk, hv, pay, hq, pay_prev, pay_next, dm,
            w_query, w_key, w_value,
        )
    with jax.named_scope("token_gradient"):
        grad, loss = band_grad(dx, base, w_query, w_key, w_value)
    full = (levels, rows, cols, width)
    return (mixed.reshape(full), grad.reshape(full), loss.reshape(()))


def solution(mesh):
    spec = P(None, "lat", "lon", None)
    return jax.shard_map(
        per_device,
        mesh=mesh,
        in_specs=(spec, spec, P(), P(), P(), P(), P(), P()),
        out_specs=(spec, spec, P()),
        check_vma=False,
    )
```
